512 devices in a mesh: wide: 64 (over x, z), narrow: 8 (over y, core).
Axes of the slice: x: 4, y: 4, z: 16, core: 2. Of those that a mesh axis runs over, the one named last changes fastest.
Arguments:
- user_feats: bfloat16 [131072, 512], P(('wide', 'narrow'))
- tower_weight: bfloat16 [512, 256], replicated, may hold values from -0.25 to 0.25
- table: float32 [65536, 256], P('wide'), may hold values from -0.4 to 0.4
- accum: float32 [65536], P('wide'), may hold values from 1 to 100
- neg_ids: int32 [2048], P('wide'), may hold values from 0 to 65535, as said below
- negative_counts: int32 [64], P('wide'), may hold values from 1 to 32, as said below
- negative_log_prob: bfloat16 [2048], P('wide'), may hold values from -12 to -4
- pos_slot: int32 [131072], P(('wide', 'narrow')), may hold values from 0 to 2047, as said below
Outputs:
- new_table: float32 [65536, 256], P('wide')
- new_accum: float32 [65536], P('wide')
- tower_grad: float32 [512, 256], replicated
The draws below stay inside these ranges and needn't reach their ends.
Inputs may be any that keep to these rules, and one draw needn't show every extreme that they name: `neg_ids`: slots w * 32 to (w + 1) * 32 - 1 hold distinct ids of rows w * 1024 to (w + 1) * 1024 - 1, the rows that owner w holds. `negative_counts`: the last owner has all 32 slots live in every draw. `pos_slot`: every query's positive is a live slot.
All inputs are finite; a program needn't handle non-finite values.
Results may differ from the reference program's by a relative error of at most 0.0073.
The reference program's roundings to bfloat16 on the way count: a program that leaves them out, or rounds other values in their place, can miss the bound.
Values may be sent and summed in bfloat16 or wider, within the bound.
No kernel may reach another device: no remote copies, remote signals or barrier semaphores. Data moves between devices by JAX's collectives and lax.ppermute only.
A program may use at most 64 MiB of HBM per device.

```python
import math
import jax
import jax.numpy as jnp
from jax import lax

EMBED_WIDTH = 256
TOWER_INPUT_WIDTH = 512
R_DEV = 1024
OWNER_SLOT_LIMIT = 32
QUERIES = 131072
TABLE_ROWS = 65536
NEGATIVE_SLOTS = 2048
N_WIDE = 64


def owner_counts(key):
    count_key = jax.random.fold_in(key, 11)
    full_key = jax.random.fold_in(key, 12)
    counts = jax.random.randint(count_key, (N_WIDE,), 1, OWNER_SLOT_LIMIT + 1)
    chosen = jax.random.randint(full_key, (), 0, N_WIDE)
    owners = jnp.arange(N_WIDE)
    full = (owners == chosen) | (owners == N_WIDE - 1)
    return jnp.where(full, OWNER_SLOT_LIMIT, counts).astype(jnp.int32)


def draw_negative_counts(key, part):
    return owner_counts(key)


def owner_picks(pick_key):
    perm_key, order_key = jax.random.split(pick_key)
    middle = jax.random.permutation(perm_key, R_DEV - 2)[:OWNER_SLOT_LIMIT - 2] + 1
    picked_slots = jnp.concatenate([jnp.array([0, R_DEV - 1], jnp.int32), middle.astype(jnp.int32)])
    return jax.random.permutation(order_key, picked_slots)


def draw_neg_ids(key, part):
    key = jax.random.fold_in(key, 3)
    keys = jax.random.split(key, N_WIDE)
    picked_slots = jax.vmap(owner_picks)(keys)
    picked_slots = picked_slots + jnp.arange(N_WIDE)[:, None] * R_DEV
    return picked_slots.reshape(NEGATIVE_SLOTS).astype(jnp.int32)


def draw_pos_slot(key, part):
    counts = owner_counts(key)
    key = jax.random.fold_in(key, 5)
    owner_key, row_key, first_key, second_key = jax.random.split(key, 4)
    owner = jax.random.randint(owner_key, (QUERIES,), 0, N_WIDE)
    offset = jax.random.randint(row_key, (QUERIES,), 0, counts[owner])
    negative_slot_rows = (owner * OWNER_SLOT_LIMIT + offset).astype(jnp.int32)
    first = jax.random.randint(first_key, (), 0, QUERIES)
    second_phase = (first + 1 + jax.random.randint(second_key, (), 0, QUERIES - 1)) % QUERIES
    slot_index = jnp.arange(QUERIES)
    negative_slot_rows = jnp.where(slot_index == first, 0, negative_slot_rows)
    negative_slot_rows = jnp.where(slot_index == second_phase, NEGATIVE_SLOTS - 1, negative_slot_rows)
    return negative_slot_rows.astype(jnp.int32)


def draw_user_feats(key, part):
    key = jax.random.fold_in(key, 7)
    value_key = jax.random.fold_in(key, 0)
    values = jnp.clip(jax.random.normal(value_key, (QUERIES, TOWER_INPUT_WIDTH), jnp.float32), -6.0, 6.0)
    return values.astype(jnp.bfloat16)


def level_of(rng, extent, pieces, smallest, largest):
    def one(axis_at, parts):
        draws = jax.random.uniform(jax.random.fold_in(jax.random.fold_in(rng, 6), axis_at), (parts,), jnp.float32, smallest / len(pieces), largest / len(pieces))
        return jnp.repeat(jnp.exp(draws), extent[axis_at] // parts).reshape((-1,) + (1,) * (len(extent) - axis_at - 1))

    factor_of = one(*pieces[0])
    for cut in pieces[1:]:
        factor_of = factor_of * one(*cut)
    return factor_of


def scatter_about(rng, extent, spread, most, cuts=(), kind=jnp.bfloat16):
    entries = jax.random.normal(rng, extent, jnp.float32) * spread
    if len(cuts) > 0:
        entries = level_of(rng, extent, cuts, -0.22, 0.18) * entries
    return jnp.clip(entries, min=-most, max=most).astype(kind)


def setup_inputs(seed: int = 0) -> dict:
    key_of = jax.random.split(jax.random.key(seed), 9)
    return {
        "user_feats": draw_user_feats(jax.random.fold_in(key_of[8], 71), 0),
        "tower_weight": scatter_about(key_of[1], (TOWER_INPUT_WIDTH, EMBED_WIDTH), TOWER_INPUT_WIDTH ** -0.5, 0.25),
        "table": scatter_about(key_of[2], (TABLE_ROWS, EMBED_WIDTH), 0.0625, 0.4, ((0, 64),), jnp.float32),
        "accum": jnp.clip(jnp.exp(math.log(100.0) - 4.6051702 * jax.random.uniform(key_of[3], (TABLE_ROWS,), jnp.float32) ** level_of(key_of[3], (TABLE_ROWS,), ((0, 64),), -0.2, 0.2)), 1.0, 100.0),
        "neg_ids": draw_neg_ids(jax.random.fold_in(key_of[8], 71), 0),
        "negative_counts": draw_negative_counts(jax.random.fold_in(key_of[8], 71), 0),
        "negative_log_prob": jnp.clip(-12.0 + 8.0 * jax.random.uniform(key_of[6], (NEGATIVE_SLOTS,), jnp.float32) ** level_of(key_of[6], (NEGATIVE_SLOTS,), ((0, 64),), -0.2, 0.2), -12.0, -4.0).astype(jnp.bfloat16),
        "pos_slot": draw_pos_slot(jax.random.fold_in(key_of[8], 71), 0),
    }


sharpness_divisor = 0.5
learn_rate = 0.05

def reference(user_feats, tower_weight, table, accum, neg_ids, negative_counts, negative_log_prob, pos_slot):
    live_mask = (jnp.arange(OWNER_SLOT_LIMIT)[None, :] < negative_counts[:, None]).reshape(NEGATIVE_SLOTS)
    item_entry_matrix = table[neg_ids].astype(jnp.bfloat16)
    position_displacement = jnp.where(live_mask, negative_log_prob, jnp.full_like(negative_log_prob, 1e+30)).astype(jnp.float32)
    block = math.gcd(QUERIES, 4096)
    feats = user_feats.reshape(QUERIES // block, block, TOWER_INPUT_WIDTH)
    negative_slot_rows = pos_slot.reshape(QUERIES // block, block)

    def step(carry, inputs):
        contrast_item_derivative, tower_grad = carry
        feat, positive_rows = inputs
        request_embeddings = jnp.dot(feat, tower_weight, preferred_element_type=jnp.float32).astype(jnp.bfloat16)
        similarity_matrix = jnp.dot(request_embeddings, item_entry_matrix.T, preferred_element_type=jnp.float32) / sharpness_divisor - position_displacement[None, :]
        top = lax.optimization_barrier(jnp.max(similarity_matrix, axis=1, keepdims=True))
        expo = jnp.exp(similarity_matrix - top)
        prob = expo / lax.optimization_barrier(jnp.sum(expo, axis=1, keepdims=True))
        slot_matched = (positive_rows[:, None] == jnp.arange(NEGATIVE_SLOTS)[None, :]).astype(jnp.float32)
        similarity_derivative = (prob - slot_matched).astype(jnp.bfloat16)
        request_vector_derivative = (jnp.dot(similarity_derivative, item_entry_matrix, preferred_element_type=jnp.float32) / sharpness_divisor).astype(jnp.bfloat16)
        tower_grad = tower_grad + jnp.dot(feat.T, request_vector_derivative, preferred_element_type=jnp.float32)
        contrast_item_derivative = contrast_item_derivative + jnp.dot(similarity_derivative.T, request_embeddings, preferred_element_type=jnp.float32) / sharpness_divisor
        return ((contrast_item_derivative, tower_grad), None)
    initial_state = (jnp.zeros((NEGATIVE_SLOTS, EMBED_WIDTH), jnp.float32), jnp.zeros((TOWER_INPUT_WIDTH, EMBED_WIDTH), jnp.float32))
    (contrast_item_derivative, tower_grad), _ = lax.scan(step, initial_state, (feats, negative_slot_rows))
    row_grad = jnp.zeros((TABLE_ROWS, EMBED_WIDTH), jnp.float32).at[neg_ids].add(contrast_item_derivative)
    new_accum = accum + lax.optimization_barrier(jnp.mean(row_grad * row_grad, axis=1))
    new_table = table - learn_rate * row_grad / jnp.sqrt(new_accum)[:, None]
    return (new_table, new_accum, tower_grad)
```

```python
import jax
import jax.numpy as jnp
from jax import lax
from jax.experimental import pallas as pl
from jax.experimental.pallas import tpu as pltpu
from jax.sharding import Mesh, PartitionSpec as P

LEARN_RATE = 0.05
X, Z, Y, CORE = 4, 16, 4, 2
NARROW = Y * CORE
PEERS = X * NARROW
PART = 4
LANES = 128
ROWS = PART * Z
F32, BF16 = jnp.float32, jnp.bfloat16


def spec(space=pltpu.VMEM):
    return pl.BlockSpec(memory_space=space)


def params(mib=16):
    return pltpu.CompilerParams(vmem_limit_bytes=mib * 1024 * 1024)


def pick_kernel(ids, counts, log_prob, table, out, tile, sems):
    z = lax.axis_index("z")
    narrow = lax.axis_index("y") * CORE + lax.axis_index("core")
    first = narrow * PART
    copies = []
    for i in range(PART):
        row = lax.rem(ids[first + i], table.shape[0])
        for half in range(2):
            copies.append(
                pltpu.make_async_copy(
                    table.at[pl.ds(row, 1), pl.ds(half * LANES, LANES)],
                    tile.at[pl.ds(half * PART + i, 1), :],
                    sems.at[half * PART + i],
                )
            )
            copies[-1].start()
    own = log_prob.shape[1]
    lane = lax.broadcasted_iota(jnp.int32, (8, LANES), 1)
    value = jnp.concatenate(
        [log_prob[...].astype(F32), jnp.zeros((1, LANES - own), F32)], axis=1
    )
    value = jnp.broadcast_to(value, (8, LANES))
    value = jnp.where(lane < counts[0], value, 1e30)
    value = jnp.where((lane >= first) & (lane < first + PART), value, 0.0)
    target = lax.rem(narrow, 2) * ROWS + z * PART
    value = pltpu.roll(value, lax.rem(target - first + LANES, LANES), 1)
    row_at = lax.broadcasted_iota(jnp.int32, (8, LANES), 0)
    tile[8:16, :] = jnp.where(row_at == 0, value, 0.0)
    for copy in copies:
        copy.wait()
    out[...] = jnp.broadcast_to(tile[...].astype(BF16)[None], out.shape)


def spread_kernel(got, out, tile):
    value = got[...].astype(F32)
    for z in range(Z):
        tile[z * PART : (z + 1) * PART, :] = value[z, 0:PART]
        tile[ROWS + z * PART : ROWS + (z + 1) * PART, :] = value[z, PART : 2 * PART]
    tile[2 * ROWS : 2 * ROWS + 8, :] = jnp.sum(value[:, 8:16], axis=0)
    tile[2 * ROWS + 8 : 2 * ROWS + 16, :] = jnp.zeros((8, LANES), F32)
    out[...] = jnp.broadcast_to(tile[...].astype(BF16)[None], out.shape)


def grad_kernel(feats, weight, pos, got, out, scores):
    queries = feats.shape[0]
    query = jnp.dot(feats[...], weight[...], preferred_element_type=F32).astype(BF16)
    step = 4
    block = step * ROWS
    n_blocks = PEERS // step

    def cand(t):
        left = got[t * step : (t + 1) * step, 0:ROWS, :].reshape(block, LANES)
        right = got[t * step : (t + 1) * step, ROWS : 2 * ROWS, :].reshape(block, LANES)
        return jnp.concatenate([left, right], axis=1)

    top = None
    for t in range(n_blocks):
        value = lax.dot_general(
            query, cand(t), (((1,), (1,)), ((), ())), preferred_element_type=F32
        )
        shifts = got[t * step : (t + 1) * step, 2 * ROWS : 2 * ROWS + 16, :].astype(F32)
        row = jnp.concatenate(
            [shifts[i, 0:1, :] + shifts[i + 1, 0:1, :] for i in range(0, step, 2)], axis=1
        )
        value = value * 2.0 - row
        scores[:, t * block : (t + 1) * block] = value
        part = value[:, 0:LANES]
        for i in range(1, block // LANES):
            part = jnp.maximum(part, value[:, i * LANES : (i + 1) * LANES])
        top = part if top is None else jnp.maximum(top, part)
    top = jnp.max(top, axis=1, keepdims=True)
    total = None
    for t in range(n_blocks):
        value = jnp.exp(scores[:, t * block : (t + 1) * block] - top)
        scores[:, t * block : (t + 1) * block] = value
        part = value[:, 0:LANES]
        for i in range(1, block // LANES):
            part = part + value[:, i * LANES : (i + 1) * LANES]
        total = part if total is None else total + part
    scale = 1.0 / jnp.sum(total, axis=1, keepdims=True)

    slot = pos[...]
    slot = (
        (slot & ~511) + (((slot >> 2) & 7) << 6) + (((slot >> 5) & 15) << 2) + (slot & 3)
    ).astype(F32)
    slot = jnp.concatenate(
        [
            jnp.broadcast_to(slot[i : i + 1, :], (LANES, LANES)).T
            for i in range(queries // LANES)
        ],
        axis=0,
    ).astype(jnp.int32)
    slot = jnp.concatenate([slot] * (block // LANES), axis=1)
    lane = lax.broadcasted_iota(jnp.int32, (queries, block), 1)
    dquery = jnp.zeros((queries, 2 * LANES), F32)
    for t in range(n_blocks):
        value = scores[:, t * block : (t + 1) * block] * scale
        hit = jnp.where(lane + t * block == slot, 1.0, 0.0)
        dscore = (value - hit).astype(BF16)
        dquery = dquery + jnp.dot(dscore, cand(t), preferred_element_type=F32)
        grad = lax.dot_general(
            dscore, query, (((0,), (0,)), ((), ())), preferred_element_type=F32
        ).astype(BF16)
        out[t * step : (t + 1) * step, 0:ROWS, :] = grad[:, 0:LANES].reshape(
            step, ROWS, LANES
        )
        out[t * step : (t + 1) * step, ROWS : 2 * ROWS, :] = grad[:, LANES:].reshape(
            step, ROWS, LANES
        )
    dquery = (dquery * 2.0).astype(BF16)
    tower = lax.dot_general(
        feats[...], dquery, (((0,), (0,)), ((), ())), preferred_element_type=F32
    ).astype(BF16)
    out[:, 2 * ROWS : 2 * ROWS + 16, :] = tower[:, 0:LANES].reshape(PEERS, 16, LANES)
    out[:, 2 * ROWS + 16 : 2 * ROWS + 32, :] = tower[:, LANES:].reshape(PEERS, 16, LANES)


def plane_sum_kernel(got, out, tile):
    total = got[0].astype(F32)
    for p in range(1, PEERS):
        total = total + got[p].astype(F32)
    tower = total[2 * ROWS :]
    for z in range(Z):
        tile[z, 0:PART, :] = total[z * PART : (z + 1) * PART]
        tile[z, PART : 2 * PART, :] = total[ROWS + z * PART : ROWS + (z + 1) * PART]
        tile[z, 8:40, :] = tower
        tile[z, 40:48, :] = jnp.zeros((8, LANES), F32)
    out[...] = tile[...].astype(BF16)


def z_sum_kernel(got, out):
    total = got[0].astype(F32)
    for z in range(1, Z):
        total = total + got[z].astype(F32)
    out[...] = jnp.broadcast_to(total.astype(BF16)[None], out.shape)


def update_kernel(ids, accum_at, got, table, accum, new_table, new_accum, tower, grad):
    rows = table.shape[0]
    value = got[...].astype(F32)
    tower[:, 0:LANES] = value[:, 8:24, :].reshape(PEERS * 16, LANES)
    tower[:, LANES:] = value[:, 24:40, :].reshape(PEERS * 16, LANES)
    own = lax.axis_index("x") * NARROW
    for n in range(NARROW):
        part = got[own + n].astype(F32)
        grad[n * PART : (n + 1) * PART, 0:LANES] = part[0:PART]
        grad[n * PART : (n + 1) * PART, LANES:] = part[PART : 2 * PART]
    slots = NARROW * PART
    row_grad = grad[...] * 2.0
    square = jnp.mean(row_grad * row_grad, axis=1, keepdims=True)
    at = lax.broadcasted_iota(jnp.int32, (slots, 1), 0)
    picked = [lax.rem(ids[i], rows) for i in range(slots)]
    old = jnp.zeros((slots, 1), F32)
    for i in range(slots):
        old = jnp.where(at == i, accum_at[picked[i]], old)
    new = old + square
    change = LEARN_RATE * row_grad / jnp.sqrt(new)
    new_table[...] = table[...]
    flat = (
        lax.broadcasted_iota(jnp.int32, accum.shape, 0) * LANES
        + lax.broadcasted_iota(jnp.int32, accum.shape, 1)
    )
    sums = accum[...]
    for i in range(slots):
        new_table[pl.ds(picked[i], 1), :] = (
            table[pl.ds(picked[i], 1), :] - change[i : i + 1, :]
        )
        sums = jnp.where(flat == picked[i], new[i : i + 1, :], sums)
    new_accum[...] = sums


def per_device(
    user_feats, tower_weight, table, accum, neg_ids, negative_counts, negative_log_prob, pos_slot
):
    shape = jax.ShapeDtypeStruct
    plane = ("x", "y", "core")
    smem = spec(pltpu.SMEM)
    picked = pl.pallas_call(
        pick_kernel,
        name="pick_rows",
        out_shape=shape((Z, 16, LANES), BF16),
        in_specs=[smem, smem, spec(), spec(pl.ANY)],
        out_specs=spec(),
        scratch_shapes=[pltpu.VMEM((16, LANES), F32), pltpu.SemaphoreType.DMA((8,))],
        compiler_params=params(),
    )(neg_ids, negative_counts, negative_log_prob.reshape(1, -1), table)
    picked = lax.all_to_all(picked, "z", 0, 0, tiled=True)
    sent = pl.pallas_call(
        spread_kernel,
        name="spread_rows",
        out_shape=shape((PEERS, 2 * ROWS + 16, LANES), BF16),
        in_specs=[spec()],
        out_specs=spec(),
        scratch_shapes=[pltpu.VMEM((2 * ROWS + 16, LANES), F32)],
        compiler_params=params(),
    )(picked)
    cands = lax.all_to_all(sent, plane, 0, 0, tiled=True)
    grads = pl.pallas_call(
        grad_kernel,
        name="gradients",
        out_shape=shape((PEERS, 2 * ROWS + 32, LANES), BF16),
        in_specs=[spec()] * 4,
        out_specs=spec(),
        scratch_shapes=[pltpu.VMEM((user_feats.shape[0], PEERS * ROWS), F32)],
        compiler_params=params(32),
    )(user_feats, tower_weight, pos_slot.reshape(-1, LANES), cands)
    grads = lax.all_to_all(grads, plane, 0, 0, tiled=True)
    sums = pl.pallas_call(
        plane_sum_kernel,
        name="plane_sum",
        out_shape=shape((Z, 48, LANES), BF16),
        in_specs=[spec()],
        out_specs=spec(),
        scratch_shapes=[pltpu.VMEM((Z, 48, LANES), F32)],
        compiler_params=params(),
    )(grads)
    sums = lax.all_to_all(sums, "z", 0, 0, tiled=True)
    whole = pl.pallas_call(
        z_sum_kernel,
        name="z_sum",
        out_shape=shape((PEERS, 48, LANES), BF16),
        in_specs=[spec()],
        out_specs=spec(),
        compiler_params=params(),
    )(sums)
    whole = lax.all_to_all(whole, plane, 0, 0, tiled=True)
    new_table, new_accum, tower_grad = pl.pallas_call(
        update_kernel,
        name="row_update",
        out_shape=(
            shape(table.shape, F32),
            shape((8, LANES), F32),
            shape(tower_weight.shape, F32),
        ),
        in_specs=[smem, smem, spec(), spec(), spec()],
        out_specs=(spec(), spec(), spec()),
        scratch_shapes=[pltpu.VMEM((NARROW * PART, 2 * LANES), F32)],
        compiler_params=params(),
    )(neg_ids, accum, whole, table, accum.reshape(8, LANES))
    return (new_table, new_accum.reshape(-1), tower_grad)


def solution(mesh):
    fine = Mesh(mesh.devices.reshape(X, Z, Y, CORE), ("x", "z", "y", "core"))
    wide, narrow = ("x", "z"), ("y", "core")
    return jax.shard_map(
        per_device,
        mesh=fine,
        in_specs=(
            P(wide + narrow, None),
            P(),
            P(wide, None),
            P(wide),
            P(wide),
            P(wide),
            P(wide),
            P(wide + narrow),
        ),
        out_specs=(P(wide, None), P(wide), P()),
        check_vma=False,
    )
```

```python
import jax
import jax.numpy as jnp
from jax import lax
from jax.experimental import pallas as pl
from jax.experimental.pallas import tpu as pltpu
from jax.sharding import Mesh, PartitionSpec as P

LEARN_RATE = 0.05
X, Z, Y, CORE = 4, 16, 4, 2
NARROW = Y * CORE
PEERS = X * NARROW
SQUARE = X * Y
PART = 4
LANES = 128
ROWS = PART * Z
F32, BF16 = jnp.float32, jnp.bfloat16


def spec(space=pltpu.VMEM):
    return pl.BlockSpec(memory_space=space)


def params(mib=16):
    return pltpu.CompilerParams(vmem_limit_bytes=mib * 1024 * 1024)


def pick_kernel(ids, counts, log_prob, table, out, tile, sems):
    z, y, core = lax.axis_index("z"), lax.axis_index("y"), lax.axis_index("core")
    first = (y * CORE + core) * PART
    copies = []
    for i in range(PART):
        row = lax.rem(ids[first + i], table.shape[0])
        for half in range(2):
            copies.append(
                pltpu.make_async_copy(
                    table.at[pl.ds(row, 1), pl.ds(half * LANES, LANES)],
                    tile.at[pl.ds(half * PART + i, 1), :],
                    sems.at[half * PART + i],
                )
            )
            copies[-1].start()
    own = log_prob.shape[1]
    lane = lax.broadcasted_iota(jnp.int32, (8, LANES), 1)
    value = jnp.concatenate(
        [log_prob[...].astype(F32), jnp.zeros((1, LANES - own), F32)], axis=1
    )
    value = jnp.broadcast_to(value, (8, LANES))
    value = jnp.where(lane < counts[0], value, 1e30)
    value = jnp.where((lane >= first) & (lane < first + PART), value, 0.0)
    target = lax.rem(y, 2) * ROWS + z * PART
    value = pltpu.roll(value, lax.rem(target - first + LANES, LANES), 1)
    row_at = lax.broadcasted_iota(jnp.int32, (8, LANES), 0)
    tile[8:16, :] = jnp.where(row_at == 0, value, 0.0)
    for copy in copies:
        copy.wait()
    out[...] = jnp.broadcast_to(tile[...].astype(BF16)[None], out.shape)


def spread_kernel(got, out, tile):
    value = got[...].astype(F32)
    for z in range(Z):
        tile[z * PART : (z + 1) * PART, :] = value[z, 0:PART]
        tile[ROWS + z * PART : ROWS + (z + 1) * PART, :] = value[z, PART : 2 * PART]
    tile[2 * ROWS : 2 * ROWS + 8, :] = jnp.sum(value[:, 8:16], axis=0)
    tile[2 * ROWS + 8 : 2 * ROWS + 16, :] = jnp.zeros((8, LANES), F32)
    out[...] = jnp.broadcast_to(tile[...].astype(BF16)[None], out.shape)


def grad_kernel(feats, weight, pos, mine, theirs, kept, sent, scores):
    queries = feats.shape[0]
    core = lax.axis_index("core")
    query = jnp.dot(feats[...], weight[...], preferred_element_type=F32).astype(BF16)
    step = 4
    block = step * ROWS
    half_blocks = SQUARE // step
    n_blocks = CORE * half_blocks

    def source(t):
        first = (t % half_blocks) * step
        return (mine if t < half_blocks else theirs), first

    def cand(t):
        ref, first = source(t)
        left = ref[first : first + step, 0:ROWS, :].reshape(block, LANES)
        right = ref[first : first + step, ROWS : 2 * ROWS, :].reshape(block, LANES)
        return jnp.concatenate([left, right], axis=1)

    top = None
    for t in range(n_blocks):
        ref, first = source(t)
        value = lax.dot_general(
            query, cand(t), (((1,), (1,)), ((), ())), preferred_element_type=F32
        )
        shifts = ref[first : first + step, 2 * ROWS : 2 * ROWS + 16, :].astype(F32)
        row = jnp.concatenate(
            [shifts[i, 0:1, :] + shifts[i + 1, 0:1, :] for i in range(0, step, 2)], axis=1
        )
        value = value * 2.0 - row
        scores[:, t * block : (t + 1) * block] = value
        part = value[:, 0:LANES]
        for i in range(1, block // LANES):
            part = jnp.maximum(part, value[:, i * LANES : (i + 1) * LANES])
        top = part if top is None else jnp.maximum(top, part)
    top = jnp.max(top, axis=1, keepdims=True)
    total = None
    for t in range(n_blocks):
        value = jnp.exp(scores[:, t * block : (t + 1) * block] - top)
        scores[:, t * block : (t + 1) * block] = value
        part = value[:, 0:LANES]
        for i in range(1, block // LANES):
            part = part + value[:, i * LANES : (i + 1) * LANES]
        total = part if total is None else total + part
    scale = 1.0 / jnp.sum(total, axis=1, keepdims=True)

    slot = pos[...]
    other = jnp.where(((slot >> 2) & 1) == core, 0, SQUARE * ROWS)
    slot = (
        other
        + ((slot >> 9) << 8)
        + (((slot >> 3) & 3) << 6)
        + (((slot >> 5) & 15) << 2)
        + (slot & 3)
    ).astype(F32)
    slot = jnp.concatenate(
        [
            jnp.broadcast_to(slot[i : i + 1, :], (LANES, LANES)).T
            for i in range(queries // LANES)
        ],
        axis=0,
    ).astype(jnp.int32)
    slot = jnp.concatenate([slot] * (block // LANES), axis=1)
    lane = lax.broadcasted_iota(jnp.int32, (queries, block), 1)
    dquery = jnp.zeros((queries, 2 * LANES), F32)
    for t in range(n_blocks):
        value = scores[:, t * block : (t + 1) * block] * scale
        hit = jnp.where(lane + t * block == slot, 1.0, 0.0)
        dscore = (value - hit).astype(BF16)
        dquery = dquery + jnp.dot(dscore, cand(t), preferred_element_type=F32)
        grad = lax.dot_general(
            dscore, query, (((0,), (0,)), ((), ())), preferred_element_type=F32
        )
        _, first = source(t)
        ref = kept if t < half_blocks else sent
        for half in range(2):
            ref[first : first + step, half * ROWS : (half + 1) * ROWS, :] = (
                grad[:, half * LANES : (half + 1) * LANES]
                .reshape(step, ROWS, LANES)
                .astype(ref.dtype)
            )
    dquery = (dquery * 2.0).astype(BF16)
    tower = lax.dot_general(
        feats[...], dquery, (((0,), (0,)), ((), ())), preferred_element_type=F32
    )
    for half in range(2):
        part = tower[:, half * LANES : (half + 1) * LANES].reshape(SQUARE, CORE, 16, LANES)
        low, high = part[:, 0], part[:, 1]
        rows = slice(2 * ROWS + half * 16, 2 * ROWS + half * 16 + 16)
        kept[:, rows, :] = jnp.where(core == 0, low, high)
        sent[:, rows, :] = jnp.where(core == 0, high, low).astype(BF16)


def chip_sum_kernel(kept, got, out):
    out[...] = (kept[...] + got[...].astype(F32)).astype(BF16)


def plane_sum_kernel(got, out, tile):
    total = got[0].astype(F32)
    for p in range(1, SQUARE):
        total = total + got[p].astype(F32)
    tower = total[2 * ROWS :]
    for z in range(Z):
        tile[z, 0:PART, :] = total[z * PART : (z + 1) * PART]
        tile[z, PART : 2 * PART, :] = total[ROWS + z * PART : ROWS + (z + 1) * PART]
        tile[z, 8:40, :] = tower
        tile[z, 40:48, :] = jnp.zeros((8, LANES), F32)
    out[...] = tile[...].astype(BF16)


def z_sum_kernel(got, out):
    total = got[0].astype(F32)
    for z in range(1, Z):
        total = total + got[z].astype(F32)
    out[...] = jnp.broadcast_to(total.astype(BF16)[None], out.shape)


def update_kernel(
    ids, accum_at, got, table, accum, new_table, new_accum, tower, grad
):
    rows = table.shape[0]
    value = got[...].astype(F32)
    tower[:, 0:LANES] = value[:, 8:24, :].reshape(PEERS * 16, LANES)
    tower[:, LANES:] = value[:, 24:40, :].reshape(PEERS * 16, LANES)
    own = lax.axis_index("x") * NARROW
    for n in range(NARROW):
        part = got[own + n].astype(F32)
        grad[n * PART : (n + 1) * PART, 0:LANES] = part[0:PART]
        grad[n * PART : (n + 1) * PART, LANES:] = part[PART : 2 * PART]
    slots = NARROW * PART
    row_grad = grad[...] * 2.0
    square = jnp.mean(row_grad * row_grad, axis=1, keepdims=True)
    at = lax.broadcasted_iota(jnp.int32, (slots, 1), 0)
    picked = [lax.rem(ids[i], rows) for i in range(slots)]
    old = jnp.zeros((slots, 1), F32)
    for i in range(slots):
        old = jnp.where(at == i, accum_at[picked[i]], old)
    new = old + square
    change = LEARN_RATE * row_grad / jnp.sqrt(new)
    new_table[...] = table[...]
    flat = (
        lax.broadcasted_iota(jnp.int32, accum.shape, 0) * LANES
        + lax.broadcasted_iota(jnp.int32, accum.shape, 1)
    )
    sums = accum[...]
    for i in range(slots):
        new_table[pl.ds(picked[i], 1), :] = (
            table[pl.ds(picked[i], 1), :] - change[i : i + 1, :]
        )
        sums = jnp.where(flat == picked[i], new[i : i + 1, :], sums)
    new_accum[...] = sums


def per_device(
    user_feats, tower_weight, table, accum, neg_ids, negative_counts, negative_log_prob, pos_slot
):
    shape = jax.ShapeDtypeStruct
    plane, square = ("x", "y", "core"), ("x", "y")
    smem, hbm = spec(pltpu.SMEM), spec(pltpu.HBM)
    dma = pltpu.SemaphoreType.DMA
    slots = NARROW * PART
    swap = [(0, 1), (1, 0)]
    picked = pl.pallas_call(
        pick_kernel,
        name="pick_rows",
        out_shape=shape((Z, 16, LANES), BF16),
        in_specs=[smem, smem, spec(), hbm],
        out_specs=spec(),
        scratch_shapes=[pltpu.VMEM((16, LANES), F32), dma((8,))],
        compiler_params=params(60),
    )(neg_ids, negative_counts, negative_log_prob.reshape(1, -1), table)
    picked = lax.all_to_all(picked, "z", 0, 0, tiled=True)
    spread = pl.pallas_call(
        spread_kernel,
        name="spread_rows",
        out_shape=shape((SQUARE, 2 * ROWS + 16, LANES), BF16),
        in_specs=[spec()],
        out_specs=spec(),
        scratch_shapes=[pltpu.VMEM((2 * ROWS + 16, LANES), F32)],
        compiler_params=params(),
    )(picked)
    mine = lax.all_to_all(spread, square, 0, 0, tiled=True)
    theirs = lax.ppermute(mine, "core", swap)
    grads = (SQUARE, 2 * ROWS + 32, LANES)
    kept, sent = pl.pallas_call(
        grad_kernel,
        name="gradients",
        out_shape=(
            shape(grads, F32),
            shape(grads, BF16),
        ),
        in_specs=[spec()] * 5,
        out_specs=(spec(), spec()),
        scratch_shapes=[pltpu.VMEM((user_feats.shape[0], PEERS * ROWS), F32)],
        compiler_params=params(32),
    )(user_feats, tower_weight, pos_slot.reshape(-1, LANES), mine, theirs)
    got = lax.ppermute(sent, "core", swap)
    chip = pl.pallas_call(
        chip_sum_kernel,
        name="chip_sum",
        out_shape=shape(grads, BF16),
        in_specs=[spec()] * 2,
        out_specs=spec(),
        compiler_params=params(),
    )(kept, got)
    chip = lax.all_to_all(chip, square, 0, 0, tiled=True)
    sums = pl.pallas_call(
        plane_sum_kernel,
        name="plane_sum",
        out_shape=shape((Z, 48, LANES), BF16),
        in_specs=[spec()],
        out_specs=spec(),
        scratch_shapes=[pltpu.VMEM((Z, 48, LANES), F32)],
        compiler_params=params(),
    )(chip)
    sums = lax.all_to_all(sums, "z", 0, 0, tiled=True)
    whole = pl.pallas_call(
        z_sum_kernel,
        name="z_sum",
        out_shape=shape((PEERS, 48, LANES), BF16),
        in_specs=[spec()],
        out_specs=spec(),
        compiler_params=params(),
    )(sums)
    whole = lax.all_to_all(whole, plane, 0, 0, tiled=True)
    new_table, new_accum, tower_grad = pl.pallas_call(
        update_kernel,
        name="row_update",
        out_shape=(
            shape(table.shape, F32),
            shape((8, LANES), F32),
            shape(tower_weight.shape, F32),
        ),
        in_specs=[smem, smem, spec(), spec(), spec()],
        out_specs=(spec(), spec(), spec()),
        scratch_shapes=[pltpu.VMEM((slots, 2 * LANES), F32)],
        compiler_params=params(),
    )(neg_ids, accum, whole, table, accum.reshape(8, LANES))
    return (new_table, new_accum.reshape(-1), tower_grad)


def solution(mesh):
    fine = Mesh(mesh.devices.reshape(X, Z, Y, CORE), ("x", "z", "y", "core"))
    wide, narrow = ("x", "z"), ("y", "core")
    return jax.shard_map(
        per_device,
        mesh=fine,
        in_specs=(
            P(wide + narrow, None),
            P(),
            P(wide, None),
            P(wide),
            P(wide),
            P(wide),
            P(wide),
            P(wide + narrow),
        ),
        out_specs=(P(wide, None), P(wide), P()),
        check_vma=False,
    )
```

```python
import jax
import jax.numpy as jnp
from jax import lax
from jax.experimental import pallas as pl
from jax.experimental.pallas import tpu as pltpu
from jax.sharding import Mesh, PartitionSpec as P

LEARN_RATE = 0.05
X, Z, Y, CORE = 4, 16, 4, 2
NARROW = Y * CORE
PEERS = X * NARROW
SQUARE = X * Y
PART = 4
LANES = 128
ROWS = PART * Z
STEP = 4
F32, BF16 = jnp.float32, jnp.bfloat16


def spec(space=pltpu.VMEM):
    return pl.BlockSpec(memory_space=space)


def params(mib=16):
    return pltpu.CompilerParams(vmem_limit_bytes=mib * 1024 * 1024)


def pick_kernel(ids, counts, log_prob, table, out, tile, sems):
    z, y, core = lax.axis_index("z"), lax.axis_index("y"), lax.axis_index("core")
    first = (y * CORE + core) * PART
    copies = []
    for i in range(PART):
        row = lax.rem(ids[first + i], table.shape[0])
        for half in range(2):
            copies.append(
                pltpu.make_async_copy(
                    table.at[pl.ds(row, 1), pl.ds(half * LANES, LANES)],
                    tile.at[pl.ds(half * PART + i, 1), :],
                    sems.at[half * PART + i],
                )
            )
            copies[-1].start()
    own = log_prob.shape[1]
    lane = lax.broadcasted_iota(jnp.int32, (8, LANES), 1)
    value = jnp.concatenate(
        [log_prob[...].astype(F32), jnp.zeros((1, LANES - own), F32)], axis=1
    )
    value = jnp.broadcast_to(value, (8, LANES))
    value = jnp.where(lane < counts[0], value, 1e30)
    value = jnp.where((lane >= first) & (lane < first + PART), value, 0.0)
    target = lax.rem(y, 2) * ROWS + z * PART
    value = pltpu.roll(value, lax.rem(target - first + LANES, LANES), 1)
    row_at = lax.broadcasted_iota(jnp.int32, (8, LANES), 0)
    tile[8:16, :] = jnp.where(row_at == 0, value, 0.0)
    for copy in copies:
        copy.wait()
    out[...] = jnp.broadcast_to(tile[...].astype(BF16)[None], out.shape)


def spread_kernel(got, out, tile):
    value = got[...].astype(F32)
    for z in range(Z):
        tile[z * PART : (z + 1) * PART, :] = value[z, 0:PART]
        tile[ROWS + z * PART : ROWS + (z + 1) * PART, :] = value[z, PART : 2 * PART]
    tile[2 * ROWS : 2 * ROWS + 8, :] = jnp.sum(value[:, 8:16], axis=0)
    tile[2 * ROWS + 8 : 2 * ROWS + 16, :] = jnp.zeros((8, LANES), F32)
    out[...] = jnp.broadcast_to(tile[...].astype(BF16)[None], out.shape)


def cand_block(got, first, count):
    left = got[first : first + count, 0:ROWS, :].reshape(count * ROWS, LANES)
    right = got[first : first + count, ROWS : 2 * ROWS, :].reshape(count * ROWS, LANES)
    return jnp.concatenate([left, right], axis=1)


def query_kernel(feats, feats2, weight, query):
    queries = feats.shape[0]
    query[0:queries, :] = jnp.dot(
        feats[...], weight[...], preferred_element_type=F32
    ).astype(BF16)
    query[queries:, :] = jnp.dot(
        feats2[...], weight[...], preferred_element_type=F32
    ).astype(BF16)


def score_kernel(query, pos, got, expo, columns, stats):
    blocks = query.shape[0] // LANES
    block = STEP * ROWS
    top = None
    for t in range(SQUARE // STEP):
        first = t * STEP
        value = lax.dot_general(
            query[...],
            cand_block(got, first, STEP),
            (((1,), (1,)), ((), ())),
            preferred_element_type=F32,
        )
        shifts = got[first : first + STEP, 2 * ROWS : 2 * ROWS + 16, :].astype(F32)
        row = jnp.concatenate(
            [shifts[i, 0:1, :] + shifts[i + 1, 0:1, :] for i in range(0, STEP, 2)], axis=1
        )
        value = value * 2.0 - row
        expo[:, t * block : (t + 1) * block] = value
        part = value[:, 0:LANES]
        for i in range(1, block // LANES):
            part = jnp.maximum(part, value[:, i * LANES : (i + 1) * LANES])
        top = part if top is None else jnp.maximum(top, part)
    top = jnp.max(top, axis=1, keepdims=True)
    total = None
    for t in range(SQUARE // STEP):
        value = jnp.exp(expo[:, t * block : (t + 1) * block] - top)
        expo[:, t * block : (t + 1) * block] = value
        part = value[:, 0:LANES]
        for i in range(1, block // LANES):
            part = part + value[:, i * LANES : (i + 1) * LANES]
        total = part if total is None else total + part
    total = jnp.sum(total, axis=1, keepdims=True)
    lane = lax.broadcasted_iota(jnp.int32, (blocks * LANES, LANES), 1)
    both = jnp.where(lane == 0, top, total)
    columns[...] = both
    rows = [both[i * LANES : (i + 1) * LANES].T for i in range(blocks)]
    stats[0:blocks, :] = jnp.concatenate([row[0:1] for row in rows], axis=0)
    stats[blocks : 2 * blocks, :] = jnp.concatenate([row[1:2] for row in rows], axis=0)
    slot = pos[...]
    slot = (
        (((slot >> 2) & 1) << 10)
        + ((slot >> 9) << 8)
        + (((slot >> 3) & 3) << 6)
        + (((slot >> 5) & 15) << 2)
        + (slot & 3)
    ).astype(F32)
    pad = jnp.zeros((stats.shape[0] - 2 * blocks - slot.shape[0], LANES), F32)
    stats[2 * blocks :, :] = jnp.concatenate([slot, pad], axis=0)


def tower_kernel(feats, feats2, got, expo, columns, stats, dscore, kept, sent):
    queries = feats.shape[0]
    block = STEP * ROWS
    blocks = 2 * queries // LANES
    core = lax.axis_index("core")
    mine, theirs = stats[core], stats[1 - core]
    tiles = []
    for i in range(blocks):
        other = (i + blocks // 2) % blocks
        owner = mine if i < blocks // 2 else theirs
        at = 2 * blocks + i % (blocks // 2)
        tile = [
            theirs[other : other + 1],
            theirs[blocks + other : blocks + other + 1],
            owner[at : at + 1],
            jnp.zeros((5, LANES), F32),
        ]
        tiles.append(jnp.concatenate(tile, axis=0).T)
    tiles = jnp.concatenate(tiles, axis=0)
    top1, total1 = columns[:, 0:1], columns[:, 1:2]
    top2, total2, slot = tiles[:, 0:1], tiles[:, 1:2], tiles[:, 2:3]
    top = jnp.maximum(top1, top2)
    share = jnp.exp(top1 - top)
    scale = share / (total1 * share + total2 * jnp.exp(top2 - top))
    slot = slot.astype(jnp.int32) - core * (SQUARE * ROWS)
    lane = lax.broadcasted_iota(jnp.int32, (2 * queries, block), 1)
    dquery = jnp.zeros((2 * queries, 2 * LANES), F32)
    for t in range(SQUARE // STEP):
        hit = jnp.where(lane == slot - t * block, 1.0, 0.0)
        value = (expo[:, t * block : (t + 1) * block] * scale - hit).astype(BF16)
        dscore[:, t * block : (t + 1) * block] = value
        dquery = dquery + jnp.dot(
            value, cand_block(got, t * STEP, STEP), preferred_element_type=F32
        )
    dquery = (dquery * 2.0).astype(BF16)
    contract = (((0,), (0,)), ((), ()))
    tower = lax.dot_general(
        feats[...], dquery[0:queries], contract, preferred_element_type=F32
    ) + lax.dot_general(feats2[...], dquery[queries:], contract, preferred_element_type=F32)
    for half in range(2):
        part = tower[:, half * LANES : (half + 1) * LANES].reshape(SQUARE, CORE, 16, LANES)
        low, high = part[:, 0], part[:, 1]
        rows = slice(half * 16, half * 16 + 16)
        kept[:, rows, :] = jnp.where(core == 0, low, high)
        sent[:, rows, :] = jnp.where(core == 0, high, low).astype(BF16)


def slot_kernel(dscore, query, out):
    block = STEP * ROWS
    for t in range(SQUARE // STEP):
        grad = lax.dot_general(
            dscore[:, t * block : (t + 1) * block],
            query[...],
            (((0,), (0,)), ((), ())),
            preferred_element_type=F32,
        ).astype(BF16)
        for half in range(2):
            out[t * STEP : (t + 1) * STEP, half * ROWS : (half + 1) * ROWS, :] = grad[
                :, half * LANES : (half + 1) * LANES
            ].reshape(STEP, ROWS, LANES)


def join_kernel(slots, kept, got, out):
    out[:, 0 : 2 * ROWS, :] = slots[...]
    out[:, 2 * ROWS :, :] = (kept[...] + got[...].astype(F32)).astype(BF16)


def plane_sum_kernel(got, out, tile):
    total = got[0].astype(F32)
    for p in range(1, SQUARE):
        total = total + got[p].astype(F32)
    tower = total[2 * ROWS :]
    for z in range(Z):
        tile[z, 0:PART, :] = total[z * PART : (z + 1) * PART]
        tile[z, PART : 2 * PART, :] = total[ROWS + z * PART : ROWS + (z + 1) * PART]
        tile[z, 8:40, :] = tower
    out[...] = tile[...].astype(BF16)


def z_sum_kernel(got, out):
    total = got[0].astype(F32)
    for z in range(1, Z):
        total = total + got[z].astype(F32)
    out[...] = jnp.broadcast_to(total.astype(BF16)[None], out.shape)


def update_kernel(
    ids, accum_at, got, table, accum, new_table, new_accum, tower, grad
):
    rows = table.shape[0]
    value = got[...].astype(F32)
    tower[:, 0:LANES] = value[:, 8:24, :].reshape(PEERS * 16, LANES)
    tower[:, LANES:] = value[:, 24:40, :].reshape(PEERS * 16, LANES)
    own = lax.axis_index("x") * NARROW
    for n in range(NARROW):
        part = got[own + n].astype(F32)
        grad[n * PART : (n + 1) * PART, 0:LANES] = part[0:PART]
        grad[n * PART : (n + 1) * PART, LANES:] = part[PART : 2 * PART]
    slots = NARROW * PART
    row_grad = grad[...] * 2.0
    square = jnp.mean(row_grad * row_grad, axis=1, keepdims=True)
    at = lax.broadcasted_iota(jnp.int32, (slots, 1), 0)
    picked = [lax.rem(ids[i], rows) for i in range(slots)]
    old = jnp.zeros((slots, 1), F32)
    for i in range(slots):
        old = jnp.where(at == i, accum_at[picked[i]], old)
    new = old + square
    change = LEARN_RATE * row_grad / jnp.sqrt(new)
    new_table[...] = table[...]
    flat = (
        lax.broadcasted_iota(jnp.int32, accum.shape, 0) * LANES
        + lax.broadcasted_iota(jnp.int32, accum.shape, 1)
    )
    sums = accum[...]
    for i in range(slots):
        new_table[pl.ds(picked[i], 1), :] = (
            table[pl.ds(picked[i], 1), :] - change[i : i + 1, :]
        )
        sums = jnp.where(flat == picked[i], new[i : i + 1, :], sums)
    new_accum[...] = sums


def per_device(
    user_feats, tower_weight, table, accum, neg_ids, negative_counts, negative_log_prob, pos_slot
):
    shape = jax.ShapeDtypeStruct
    plane, square = ("x", "y", "core"), ("x", "y")
    smem, hbm = spec(pltpu.SMEM), spec(pltpu.HBM)
    dma = pltpu.SemaphoreType.DMA
    slots = NARROW * PART
    swap = [(0, 1), (1, 0)]
    picked = pl.pallas_call(
        pick_kernel,
        name="pick_rows",
        out_shape=shape((Z, 16, LANES), BF16),
        in_specs=[smem, smem, spec(), hbm],
        out_specs=spec(),
        scratch_shapes=[pltpu.VMEM((16, LANES), F32), dma((8,))],
        compiler_params=params(60),
    )(neg_ids, negative_counts, negative_log_prob.reshape(1, -1), table)
    picked = lax.all_to_all(picked, "z", 0, 0, tiled=True)
    spread = pl.pallas_call(
        spread_kernel,
        name="spread_rows",
        out_shape=shape((SQUARE, 2 * ROWS + 16, LANES), BF16),
        in_specs=[spec()],
        out_specs=spec(),
        scratch_shapes=[pltpu.VMEM((2 * ROWS + 16, LANES), F32)],
        compiler_params=params(),
    )(picked)
    mine = lax.all_to_all(spread, square, 0, 0, tiled=True)
    queries = user_feats.shape[0]
    half_slots = SQUARE * ROWS
    feats2 = lax.ppermute(user_feats, "core", swap)
    query = pl.pallas_call(
        query_kernel,
        name="queries",
        out_shape=shape((2 * queries, 2 * LANES), BF16),
        in_specs=[spec()] * 3,
        out_specs=spec(),
        compiler_params=params(),
        cost_estimate=pl.CostEstimate(
            flops=16 * queries * LANES * 4 * LANES, bytes_accessed=2**20, transcendentals=0
        ),
    )(user_feats, feats2, tower_weight)
    expo, columns, stats = pl.pallas_call(
        score_kernel,
        name="scores",
        out_shape=(
            shape((2 * queries, half_slots), F32),
            shape((2 * queries, LANES), F32),
            shape((16, LANES), F32),
        ),
        in_specs=[spec()] * 3,
        out_specs=(spec(),) * 3,
        compiler_params=params(32),
    )(query, pos_slot.reshape(-1, LANES), mine)
    stats = lax.all_gather(stats, "core", axis=0)
    tower_part = (SQUARE, 32, LANES)
    dscore, kept, sent = pl.pallas_call(
        tower_kernel,
        name="tower_gradient",
        out_shape=(
            shape((2 * queries, half_slots), BF16),
            shape(tower_part, F32),
            shape(tower_part, BF16),
        ),
        in_specs=[spec()] * 6,
        out_specs=(spec(),) * 3,
        compiler_params=params(32),
    )(user_feats, feats2, mine, expo, columns, stats)
    got = lax.ppermute(sent, "core", swap)
    slot_part = pl.pallas_call(
        slot_kernel,
        name="slot_gradient",
        out_shape=shape((SQUARE, 2 * ROWS, LANES), BF16),
        in_specs=[spec()] * 2,
        out_specs=spec(),
        compiler_params=params(32),
        cost_estimate=pl.CostEstimate(
            flops=8 * queries * half_slots * LANES, bytes_accessed=2**21, transcendentals=0
        ),
    )(dscore, query)
    chip = pl.pallas_call(
        join_kernel,
        name="join_tower",
        out_shape=shape((SQUARE, 2 * ROWS + 32, LANES), BF16),
        in_specs=[spec()] * 3,
        out_specs=spec(),
        compiler_params=params(),
    )(slot_part, kept, got)
    chip = lax.all_to_all(chip, square, 0, 0, tiled=True)
    sums = pl.pallas_call(
        plane_sum_kernel,
        name="plane_sum",
        out_shape=shape((Z, 40, LANES), BF16),
        in_specs=[spec()],
        out_specs=spec(),
        scratch_shapes=[pltpu.VMEM((Z, 40, LANES), F32)],
        compiler_params=params(),
    )(chip)
    sums = lax.all_to_all(sums, "z", 0, 0, tiled=True)
    whole = pl.pallas_call(
        z_sum_kernel,
        name="z_sum",
        out_shape=shape((PEERS, 40, LANES), BF16),
        in_specs=[spec()],
        out_specs=spec(),
        compiler_params=params(),
    )(sums)
    whole = lax.all_to_all(whole, plane, 0, 0, tiled=True)
    new_table, new_accum, tower_grad = pl.pallas_call(
        update_kernel,
        name="row_update",
        out_shape=(
            shape(table.shape, F32),
            shape((8, LANES), F32),
            shape(tower_weight.shape, F32),
        ),
        in_specs=[smem, smem, spec(), spec(), spec()],
        out_specs=(spec(), spec(), spec()),
        scratch_shapes=[pltpu.VMEM((slots, 2 * LANES), F32)],
        compiler_params=params(),
    )(neg_ids, accum, whole, table, accum.reshape(8, LANES))
    return (new_table, new_accum.reshape(-1), tower_grad)


def solution(mesh):
    fine = Mesh(mesh.devices.reshape(X, Z, Y, CORE), ("x", "z", "y", "core"))
    wide, narrow = ("x", "z"), ("y", "core")
    return jax.shard_map(
        per_device,
        mesh=fine,
        in_specs=(
            P(wide + narrow, None),
            P(),
            P(wide, None),
            P(wide),
            P(wide),
            P(wide),
            P(wide),
            P(wide + narrow),
        ),
        out_specs=(P(wide, None), P(wide), P()),
        check_vma=False,
    )
```

```python
import jax
import jax.numpy as jnp
from jax import lax
from jax.experimental import pallas as pl
from jax.experimental.pallas import tpu as pltpu
from jax.sharding import Mesh, PartitionSpec as P

LEARN_RATE = 0.05
X, Z, Y, CORE = 4, 16, 4, 2
NARROW = Y * CORE
PEERS = X * NARROW
SQUARE = X * Y
PART = 4
LANES = 128
ROWS = PART * Z
STEP = 4
F32, BF16 = jnp.float32, jnp.bfloat16


def spec(space=pltpu.VMEM):
    return pl.BlockSpec(memory_space=space)


def params(mib=16):
    return pltpu.CompilerParams(vmem_limit_bytes=mib * 1024 * 1024)


def pick_kernel(ids, counts, log_prob, table, out, tile, sems):
    z, y, core = lax.axis_index("z"), lax.axis_index("y"), lax.axis_index("core")
    first = (y * CORE + core) * PART
    copies = []
    for i in range(PART):
        row = lax.rem(ids[first + i], table.shape[0])
        for half in range(2):
            copies.append(
                pltpu.make_async_copy(
                    table.at[pl.ds(row, 1), pl.ds(half * LANES, LANES)],
                    tile.at[pl.ds(half * PART + i, 1), :],
                    sems.at[half * PART + i],
                )
            )
            copies[-1].start()
    own = log_prob.shape[1]
    lane = lax.broadcasted_iota(jnp.int32, (8, LANES), 1)
    value = jnp.concatenate(
        [log_prob[...].astype(F32), jnp.zeros((1, LANES - own), F32)], axis=1
    )
    value = jnp.broadcast_to(value, (8, LANES))
    value = jnp.where(lane < counts[0], value, 1e30)
    value = jnp.where((lane >= first) & (lane < first + PART), value, 0.0)
    target = lax.rem(y, 2) * ROWS + z * PART
    value = pltpu.roll(value, lax.rem(target - first + LANES, LANES), 1)
    row_at = lax.broadcasted_iota(jnp.int32, (8, LANES), 0)
    tile[8:16, :] = jnp.where(row_at == 0, value, 0.0)
    for copy in copies:
        copy.wait()
    out[...] = jnp.broadcast_to(tile[...].astype(BF16)[None], out.shape)


def spread_kernel(got, out, tile):
    value = got[...].astype(F32)
    for z in range(Z):
        tile[z * PART : (z + 1) * PART, :] = value[z, 0:PART]
        tile[ROWS + z * PART : ROWS + (z + 1) * PART, :] = value[z, PART : 2 * PART]
    tile[2 * ROWS : 2 * ROWS + 8, :] = jnp.sum(value[:, 8:16], axis=0)
    tile[2 * ROWS + 8 : 2 * ROWS + 16, :] = jnp.zeros((8, LANES), F32)
    out[...] = jnp.broadcast_to(tile[...].astype(BF16)[None], out.shape)


def cand_block(got, first, count):
    left = got[first : first + count, 0:ROWS, :].reshape(count * ROWS, LANES)
    right = got[first : first + count, ROWS : 2 * ROWS, :].reshape(count * ROWS, LANES)
    return jnp.concatenate([left, right], axis=1)


def query_kernel(feats, feats2, weight, query):
    queries = feats.shape[0]
    query[0:queries, :] = jnp.dot(
        feats[...], weight[...], preferred_element_type=F32
    ).astype(BF16)
    query[queries:, :] = jnp.dot(
        feats2[...], weight[...], preferred_element_type=F32
    ).astype(BF16)


def score_kernel(query, pos, got, expo, columns, stats):
    blocks = query.shape[0] // LANES
    block = STEP * ROWS
    top = None
    for t in range(SQUARE // STEP):
        first = t * STEP
        value = lax.dot_general(
            query[...],
            cand_block(got, first, STEP),
            (((1,), (1,)), ((), ())),
            preferred_element_type=F32,
        )
        shifts = got[first : first + STEP, 2 * ROWS : 2 * ROWS + 16, :].astype(F32)
        row = jnp.concatenate(
            [shifts[i, 0:1, :] + shifts[i + 1, 0:1, :] for i in range(0, STEP, 2)], axis=1
        )
        value = value * 2.0 - row
        expo[:, t * block : (t + 1) * block] = value
        part = value[:, 0:LANES]
        for i in range(1, block // LANES):
            part = jnp.maximum(part, value[:, i * LANES : (i + 1) * LANES])
        top = part if top is None else jnp.maximum(top, part)
    top = jnp.max(top, axis=1, keepdims=True)
    total = None
    for t in range(SQUARE // STEP):
        value = jnp.exp(expo[:, t * block : (t + 1) * block] - top)
        expo[:, t * block : (t + 1) * block] = value
        part = value[:, 0:LANES]
        for i in range(1, block // LANES):
            part = part + value[:, i * LANES : (i + 1) * LANES]
        total = part if total is None else total + part
    total = jnp.sum(total, axis=1, keepdims=True)
    lane = lax.broadcasted_iota(jnp.int32, (blocks * LANES, LANES), 1)
    both = jnp.where(lane == 0, top, total)
    columns[...] = both
    rows = [both[i * LANES : (i + 1) * LANES].T for i in range(blocks)]
    stats[0:blocks, :] = jnp.concatenate([row[0:1] for row in rows], axis=0)
    stats[blocks : 2 * blocks, :] = jnp.concatenate([row[1:2] for row in rows], axis=0)
    slot = pos[...]
    slot = (
        (((slot >> 2) & 1) << 10)
        + ((slot >> 9) << 8)
        + (((slot >> 3) & 3) << 6)
        + (((slot >> 5) & 15) << 2)
        + (slot & 3)
    ).astype(F32)
    pad = jnp.zeros((stats.shape[0] - 2 * blocks - slot.shape[0], LANES), F32)
    stats[2 * blocks :, :] = jnp.concatenate([slot, pad], axis=0)


def tower_kernel(feats, feats2, got, expo, columns, stats, dscore, kept, sent):
    queries = feats.shape[0]
    block = STEP * ROWS
    blocks = 2 * queries // LANES
    core = lax.axis_index("core")
    mine, theirs = stats[core], stats[1 - core]
    tiles = []
    for i in range(blocks):
        other = (i + blocks // 2) % blocks
        owner = mine if i < blocks // 2 else theirs
        at = 2 * blocks + i % (blocks // 2)
        tile = [
            theirs[other : other + 1],
            theirs[blocks + other : blocks + other + 1],
            owner[at : at + 1],
            jnp.zeros((5, LANES), F32),
        ]
        tiles.append(jnp.concatenate(tile, axis=0).T)
    tiles = jnp.concatenate(tiles, axis=0)
    top1, total1 = columns[:, 0:1], columns[:, 1:2]
    top2, total2, slot = tiles[:, 0:1], tiles[:, 1:2], tiles[:, 2:3]
    top = jnp.maximum(top1, top2)
    share = jnp.exp(top1 - top)
    scale = share / (total1 * share + total2 * jnp.exp(top2 - top))
    slot = slot.astype(jnp.int32) - core * (SQUARE * ROWS)
    lane = lax.broadcasted_iota(jnp.int32, (2 * queries, block), 1)
    dquery = jnp.zeros((2 * queries, 2 * LANES), F32)
    for t in range(SQUARE // STEP):
        hit = jnp.where(lane == slot - t * block, 1.0, 0.0)
        value = (expo[:, t * block : (t + 1) * block] * scale - hit).astype(BF16)
        dscore[:, t * block : (t + 1) * block] = value
        dquery = dquery + jnp.dot(
            value, cand_block(got, t * STEP, STEP), preferred_element_type=F32
        )
    dquery = (dquery * 2.0).astype(BF16)
    contract = (((0,), (0,)), ((), ()))
    tower = lax.dot_general(
        feats[...], dquery[0:queries], contract, preferred_element_type=F32
    ) + lax.dot_general(feats2[...], dquery[queries:], contract, preferred_element_type=F32)
    for half in range(2):
        part = tower[:, half * LANES : (half + 1) * LANES].reshape(SQUARE, CORE, 16, LANES)
        low, high = part[:, 0], part[:, 1]
        rows = slice(half * 16, half * 16 + 16)
        kept[:, rows, :] = jnp.where(core == 0, low, high)
        sent[:, rows, :] = jnp.where(core == 0, high, low).astype(BF16)


def slot_kernel(dscore, query, out):
    block = STEP * ROWS
    for t in range(SQUARE // STEP):
        grad = lax.dot_general(
            dscore[:, t * block : (t + 1) * block],
            query[...],
            (((0,), (0,)), ((), ())),
            preferred_element_type=F32,
        ).astype(BF16)
        for half in range(2):
            out[t * STEP : (t + 1) * STEP, half * ROWS : (half + 1) * ROWS, :] = grad[
                :, half * LANES : (half + 1) * LANES
            ].reshape(STEP, ROWS, LANES)


def join_kernel(slots, kept, got, out):
    theirs = got[1 - lax.axis_index("core")]
    out[:, 0 : 2 * ROWS, :] = slots[...]
    out[:, 2 * ROWS :, :] = (kept[...] + theirs.astype(F32)).astype(BF16)


def plane_sum_kernel(got, out, tile):
    total = got[0].astype(F32)
    for p in range(1, SQUARE):
        total = total + got[p].astype(F32)
    tower = total[2 * ROWS :]
    for z in range(Z):
        tile[z, 0:PART, :] = total[z * PART : (z + 1) * PART]
        tile[z, PART : 2 * PART, :] = total[ROWS + z * PART : ROWS + (z + 1) * PART]
        tile[z, 8:40, :] = tower
    out[...] = tile[...].astype(BF16)


def z_sum_kernel(got, out):
    total = got[0].astype(F32)
    for z in range(1, Z):
        total = total + got[z].astype(F32)
    out[...] = jnp.broadcast_to(total.astype(BF16)[None], out.shape)


def update_kernel(
    ids, accum_at, got, table, accum, new_table, new_accum, tower, grad
):
    rows = table.shape[0]
    value = got[...].astype(F32)
    tower[:, 0:LANES] = value[:, 8:24, :].reshape(PEERS * 16, LANES)
    tower[:, LANES:] = value[:, 24:40, :].reshape(PEERS * 16, LANES)
    own = lax.axis_index("x") * NARROW
    for n in range(NARROW):
        part = got[own + n].astype(F32)
        grad[n * PART : (n + 1) * PART, 0:LANES] = part[0:PART]
        grad[n * PART : (n + 1) * PART, LANES:] = part[PART : 2 * PART]
    slots = NARROW * PART
    row_grad = grad[...] * 2.0
    square = jnp.mean(row_grad * row_grad, axis=1, keepdims=True)
    at = lax.broadcasted_iota(jnp.int32, (slots, 1), 0)
    picked = [lax.rem(ids[i], rows) for i in range(slots)]
    old = jnp.zeros((slots, 1), F32)
    for i in range(slots):
        old = jnp.where(at == i, accum_at[picked[i]], old)
    new = old + square
    change = LEARN_RATE * row_grad / jnp.sqrt(new)
    new_table[...] = table[...]
    flat = (
        lax.broadcasted_iota(jnp.int32, accum.shape, 0) * LANES
        + lax.broadcasted_iota(jnp.int32, accum.shape, 1)
    )
    sums = accum[...]
    for i in range(slots):
        new_table[pl.ds(picked[i], 1), :] = (
            table[pl.ds(picked[i], 1), :] - change[i : i + 1, :]
        )
        sums = jnp.where(flat == picked[i], new[i : i + 1, :], sums)
    new_accum[...] = sums


def per_device(
    user_feats, tower_weight, table, accum, neg_ids, negative_counts, negative_log_prob, pos_slot
):
    shape = jax.ShapeDtypeStruct
    plane, square = ("x", "y", "core"), ("x", "y")
    smem, hbm = spec(pltpu.SMEM), spec(pltpu.HBM)
    dma = pltpu.SemaphoreType.DMA
    slots = NARROW * PART
    swap = [(0, 1), (1, 0)]
    picked = pl.pallas_call(
        pick_kernel,
        name="pick_rows",
        out_shape=shape((Z, 16, LANES), BF16),
        in_specs=[smem, smem, spec(), hbm],
        out_specs=spec(),
        scratch_shapes=[pltpu.VMEM((16, LANES), F32), dma((8,))],
        compiler_params=params(60),
    )(neg_ids, negative_counts, negative_log_prob.reshape(1, -1), table)
    picked = lax.all_to_all(picked, "z", 0, 0, tiled=True)
    spread = pl.pallas_call(
        spread_kernel,
        name="spread_rows",
        out_shape=shape((SQUARE, 2 * ROWS + 16, LANES), BF16),
        in_specs=[spec()],
        out_specs=spec(),
        scratch_shapes=[pltpu.VMEM((2 * ROWS + 16, LANES), F32)],
        compiler_params=params(),
    )(picked)
    mine = lax.all_to_all(spread, square, 0, 0, tiled=True)
    queries = user_feats.shape[0]
    half_slots = SQUARE * ROWS
    feats2 = lax.ppermute(user_feats, "core", swap)
    query = pl.pallas_call(
        query_kernel,
        name="queries",
        out_shape=shape((2 * queries, 2 * LANES), BF16),
        in_specs=[spec()] * 3,
        out_specs=spec(),
        compiler_params=params(),
        cost_estimate=pl.CostEstimate(
            flops=16 * queries * LANES * 4 * LANES, bytes_accessed=2**20, transcendentals=0
        ),
    )(user_feats, feats2, tower_weight)
    expo, columns, stats = pl.pallas_call(
        score_kernel,
        name="scores",
        out_shape=(
            shape((2 * queries, half_slots), F32),
            shape((2 * queries, LANES), F32),
            shape((16, LANES), F32),
        ),
        in_specs=[spec()] * 3,
        out_specs=(spec(),) * 3,
        compiler_params=params(32),
    )(query, pos_slot.reshape(-1, LANES), mine)
    stats = lax.all_gather(stats, "core", axis=0)
    tower_part = (SQUARE, 32, LANES)
    dscore, kept, sent = pl.pallas_call(
        tower_kernel,
        name="tower_gradient",
        out_shape=(
            shape((2 * queries, half_slots), BF16),
            shape(tower_part, F32),
            shape(tower_part, BF16),
        ),
        in_specs=[spec()] * 6,
        out_specs=(spec(),) * 3,
        compiler_params=params(32),
    )(user_feats, feats2, mine, expo, columns, stats)
    got = lax.all_gather(sent, "core", axis=0)
    slot_part = pl.pallas_call(
        slot_kernel,
        name="slot_gradient",
        out_shape=shape((SQUARE, 2 * ROWS, LANES), BF16),
        in_specs=[spec()] * 2,
        out_specs=spec(),
        compiler_params=params(32),
        cost_estimate=pl.CostEstimate(
            flops=8 * queries * half_slots * LANES, bytes_accessed=2**21, transcendentals=0
        ),
    )(dscore, query)
    chip = pl.pallas_call(
        join_kernel,
        name="join_tower",
        out_shape=shape((SQUARE, 2 * ROWS + 32, LANES), BF16),
        in_specs=[spec()] * 3,
        out_specs=spec(),
        compiler_params=params(),
    )(slot_part, kept, got)
    chip = lax.all_to_all(chip, square, 0, 0, tiled=True)
    sums = pl.pallas_call(
        plane_sum_kernel,
        name="plane_sum",
        out_shape=shape((Z, 40, LANES), BF16),
        in_specs=[spec()],
        out_specs=spec(),
        scratch_shapes=[pltpu.VMEM((Z, 40, LANES), F32)],
        compiler_params=params(),
    )(chip)
    sums = lax.all_to_all(sums, "z", 0, 0, tiled=True)
    whole = pl.pallas_call(
        z_sum_kernel,
        name="z_sum",
        out_shape=shape((PEERS, 40, LANES), BF16),
        in_specs=[spec()],
        out_specs=spec(),
        compiler_params=params(),
    )(sums)
    whole = lax.all_to_all(whole, plane, 0, 0, tiled=True)
    new_table, new_accum, tower_grad = pl.pallas_call(
        update_kernel,
        name="row_update",
        out_shape=(
            shape(table.shape, F32),
            shape((8, LANES), F32),
            shape(tower_weight.shape, F32),
        ),
        in_specs=[smem, smem, spec(), spec(), spec()],
        out_specs=(spec(), spec(), spec()),
        scratch_shapes=[pltpu.VMEM((slots, 2 * LANES), F32)],
        compiler_params=params(),
    )(neg_ids, accum, whole, table, accum.reshape(8, LANES))
    return (new_table, new_accum.reshape(-1), tower_grad)


def solution(mesh):
    fine = Mesh(mesh.devices.reshape(X, Z, Y, CORE), ("x", "z", "y", "core"))
    wide, narrow = ("x", "z"), ("y", "core")
    return jax.shard_map(
        per_device,
        mesh=fine,
        in_specs=(
            P(wide + narrow, None),
            P(),
            P(wide, None),
            P(wide),
            P(wide),
            P(wide),
            P(wide),
            P(wide + narrow),
        ),
        out_specs=(P(wide, None), P(wide), P()),
        check_vma=False,
    )
```

```python
import jax
import jax.numpy as jnp
from jax import lax
from jax.experimental import pallas as pl
from jax.experimental.pallas import tpu as pltpu
from jax.sharding import Mesh, PartitionSpec as P

LEARN_RATE = 0.05
X, Z, Y, CORE = 4, 16, 4, 2
NARROW = Y * CORE
PEERS = X * NARROW
SQUARE = X * Y
PART = 4
LANES = 128
ROWS = PART * Z
STEP = 4
F32, BF16 = jnp.float32, jnp.bfloat16


def spec(space=pltpu.VMEM):
    return pl.BlockSpec(memory_space=space)


def params(mib=16):
    return pltpu.CompilerParams(vmem_limit_bytes=mib * 1024 * 1024)


def pick_kernel(ids, counts, log_prob, table, out, groups, tile, sems):
    z, y, core = lax.axis_index("z"), lax.axis_index("y"), lax.axis_index("core")
    first = (y * CORE + core) * PART
    rows = [lax.rem(ids[first + i], table.shape[0]) for i in range(PART)]
    copies = []
    for i in range(PART):
        start = pl.multiple_of((rows[i] >> 3) << 3, 8)
        copies.append(
            pltpu.make_async_copy(table.at[pl.ds(start, 8), :], groups.at[i], sems.at[i])
        )
        copies[-1].start()
    own = log_prob.shape[1]
    lane = lax.broadcasted_iota(jnp.int32, (8, LANES), 1)
    value = jnp.concatenate(
        [log_prob[...].astype(F32), jnp.zeros((1, LANES - own), F32)], axis=1
    )
    value = jnp.broadcast_to(value, (8, LANES))
    value = jnp.where(lane < counts[0], value, 1e30)
    value = jnp.where((lane >= first) & (lane < first + PART), value, 0.0)
    target = lax.rem(y, 2) * ROWS + z * PART
    value = pltpu.roll(value, lax.rem(target - first + LANES, LANES), 1)
    row_at = lax.broadcasted_iota(jnp.int32, (8, LANES), 0)
    tile[8:16, :] = jnp.where(row_at == 0, value, 0.0)
    for i in range(PART):
        copies[i].wait()
        row = groups[i, pl.ds(rows[i] & 7, 1), :]
        tile[i : i + 1, :] = row[:, 0:LANES]
        tile[PART + i : PART + i + 1, :] = row[:, LANES:]
    out[...] = jnp.broadcast_to(tile[...].astype(BF16)[None], out.shape)


def spread_kernel(got, out, tile):
    value = got[...].astype(F32)
    for z in range(Z):
        tile[z * PART : (z + 1) * PART, :] = value[z, 0:PART]
        tile[ROWS + z * PART : ROWS + (z + 1) * PART, :] = value[z, PART : 2 * PART]
    tile[2 * ROWS : 2 * ROWS + 8, :] = jnp.sum(value[:, 8:16], axis=0)
    tile[2 * ROWS + 8 : 2 * ROWS + 16, :] = jnp.zeros((8, LANES), F32)
    out[...] = jnp.broadcast_to(tile[...].astype(BF16)[None], out.shape)


def cand_block(got, first, count):
    left = got[first : first + count, 0:ROWS, :].reshape(count * ROWS, LANES)
    right = got[first : first + count, ROWS : 2 * ROWS, :].reshape(count * ROWS, LANES)
    return jnp.concatenate([left, right], axis=1)


def query_kernel(feats, feats2, weight, query):
    queries = feats.shape[0]
    query[0:queries, :] = jnp.dot(
        feats[...], weight[...], preferred_element_type=F32
    ).astype(BF16)
    query[queries:, :] = jnp.dot(
        feats2[...], weight[...], preferred_element_type=F32
    ).astype(BF16)


def score_kernel(query, pos, got, expo, columns, stats):
    blocks = query.shape[0] // LANES
    block = STEP * ROWS
    top = None
    for t in range(SQUARE // STEP):
        first = t * STEP
        value = lax.dot_general(
            query[...],
            cand_block(got, first, STEP),
            (((1,), (1,)), ((), ())),
            preferred_element_type=F32,
        )
        shifts = got[first : first + STEP, 2 * ROWS : 2 * ROWS + 16, :].astype(F32)
        row = jnp.concatenate(
            [shifts[i, 0:1, :] + shifts[i + 1, 0:1, :] for i in range(0, STEP, 2)], axis=1
        )
        value = value * 2.0 - row
        expo[:, t * block : (t + 1) * block] = value
        part = value[:, 0:LANES]
        for i in range(1, block // LANES):
            part = jnp.maximum(part, value[:, i * LANES : (i + 1) * LANES])
        top = part if top is None else jnp.maximum(top, part)
    top = jnp.max(top, axis=1, keepdims=True)
    total = None
    for t in range(SQUARE // STEP):
        value = jnp.exp(expo[:, t * block : (t + 1) * block] - top)
        expo[:, t * block : (t + 1) * block] = value
        part = value[:, 0:LANES]
        for i in range(1, block // LANES):
            part = part + value[:, i * LANES : (i + 1) * LANES]
        total = part if total is None else total + part
    total = jnp.sum(total, axis=1, keepdims=True)
    lane = lax.broadcasted_iota(jnp.int32, (blocks * LANES, LANES), 1)
    both = jnp.where(lane == 0, top, total)
    columns[...] = both
    rows = [both[i * LANES : (i + 1) * LANES].T for i in range(blocks)]
    stats[0:blocks, :] = jnp.concatenate([row[0:1] for row in rows], axis=0)
    stats[blocks : 2 * blocks, :] = jnp.concatenate([row[1:2] for row in rows], axis=0)
    slot = pos[...]
    slot = (
        (((slot >> 2) & 1) << 10)
        + ((slot >> 9) << 8)
        + (((slot >> 3) & 3) << 6)
        + (((slot >> 5) & 15) << 2)
        + (slot & 3)
    ).astype(F32)
    pad = jnp.zeros((stats.shape[0] - 2 * blocks - slot.shape[0], LANES), F32)
    stats[2 * blocks :, :] = jnp.concatenate([slot, pad], axis=0)


def tower_kernel(feats, feats2, got, expo, columns, stats, dscore, kept, sent):
    queries = feats.shape[0]
    block = STEP * ROWS
    blocks = 2 * queries // LANES
    core = lax.axis_index("core")
    mine, theirs = stats[core], stats[1 - core]
    tiles = []
    for i in range(blocks):
        other = (i + blocks // 2) % blocks
        owner = mine if i < blocks // 2 else theirs
        at = 2 * blocks + i % (blocks // 2)
        tile = [
            theirs[other : other + 1],
            theirs[blocks + other : blocks + other + 1],
            owner[at : at + 1],
            jnp.zeros((5, LANES), F32),
        ]
        tiles.append(jnp.concatenate(tile, axis=0).T)
    tiles = jnp.concatenate(tiles, axis=0)
    top1, total1 = columns[:, 0:1], columns[:, 1:2]
    top2, total2, slot = tiles[:, 0:1], tiles[:, 1:2], tiles[:, 2:3]
    top = jnp.maximum(top1, top2)
    share = jnp.exp(top1 - top)
    scale = share / (total1 * share + total2 * jnp.exp(top2 - top))
    slot = slot.astype(jnp.int32) - core * (SQUARE * ROWS)
    lane = lax.broadcasted_iota(jnp.int32, (2 * queries, block), 1)
    for t in range(SQUARE // STEP):
        hit = jnp.where(lane == slot - t * block, 1.0, 0.0)
        dscore[:, t * block : (t + 1) * block] = (
            expo[:, t * block : (t + 1) * block] * scale - hit
        ).astype(BF16)
    dquery = jnp.dot(dscore[...], cand_block(got, 0, SQUARE), preferred_element_type=F32)
    dquery = (dquery * 2.0).astype(BF16)
    contract = (((0,), (0,)), ((), ()))
    tower = lax.dot_general(
        feats[...], dquery[0:queries], contract, preferred_element_type=F32
    ) + lax.dot_general(feats2[...], dquery[queries:], contract, preferred_element_type=F32)
    for half in range(2):
        part = tower[:, half * LANES : (half + 1) * LANES].reshape(SQUARE, CORE, 16, LANES)
        low, high = part[:, 0], part[:, 1]
        rows = slice(half * 16, half * 16 + 16)
        kept[:, rows, :] = jnp.where(core == 0, low, high)
        sent[:, rows, :] = jnp.where(core == 0, high, low).astype(BF16)


def slot_kernel(dscore, query, out):
    block = STEP * ROWS
    for t in range(SQUARE // STEP):
        grad = lax.dot_general(
            dscore[:, t * block : (t + 1) * block],
            query[...],
            (((0,), (0,)), ((), ())),
            preferred_element_type=F32,
        ).astype(BF16)
        for half in range(2):
            out[t * STEP : (t + 1) * STEP, half * ROWS : (half + 1) * ROWS, :] = grad[
                :, half * LANES : (half + 1) * LANES
            ].reshape(STEP, ROWS, LANES)


def join_kernel(slots, kept, got, out):
    theirs = got[1 - lax.axis_index("core")]
    out[:, 0 : 2 * ROWS, :] = slots[...]
    out[:, 2 * ROWS :, :] = (kept[...] + theirs.astype(F32)).astype(BF16)


def plane_sum_kernel(got, out, tile):
    total = got[0].astype(F32)
    for p in range(1, SQUARE):
        total = total + got[p].astype(F32)
    tower = total[2 * ROWS :]
    for z in range(Z):
        tile[z, 0:PART, :] = total[z * PART : (z + 1) * PART]
        tile[z, PART : 2 * PART, :] = total[ROWS + z * PART : ROWS + (z + 1) * PART]
        tile[z, 8:40, :] = tower
    out[...] = tile[...].astype(BF16)


def z_sum_kernel(got, out):
    total = got[0].astype(F32)
    for z in range(1, Z):
        total = total + got[z].astype(F32)
    out[...] = jnp.broadcast_to(total.astype(BF16)[None], out.shape)


def update_kernel(
    ids, accum_at, got, table, accum, new_table, new_accum, tower, grad
):
    rows = table.shape[0]
    value = got[...].astype(F32)
    tower[:, 0:LANES] = value[:, 8:24, :].reshape(PEERS * 16, LANES)
    tower[:, LANES:] = value[:, 24:40, :].reshape(PEERS * 16, LANES)
    own = lax.axis_index("x") * NARROW
    for n in range(NARROW):
        part = got[own + n].astype(F32)
        grad[n * PART : (n + 1) * PART, 0:LANES] = part[0:PART]
        grad[n * PART : (n + 1) * PART, LANES:] = part[PART : 2 * PART]
    slots = NARROW * PART
    row_grad = grad[...] * 2.0
    square = jnp.mean(row_grad * row_grad, axis=1, keepdims=True)
    at = lax.broadcasted_iota(jnp.int32, (slots, 1), 0)
    picked = [lax.rem(ids[i], rows) for i in range(slots)]
    old = jnp.zeros((slots, 1), F32)
    for i in range(slots):
        old = jnp.where(at == i, accum_at[picked[i]], old)
    new = old + square
    change = LEARN_RATE * row_grad / jnp.sqrt(new)
    new_table[...] = table[...]
    flat = (
        lax.broadcasted_iota(jnp.int32, accum.shape, 0) * LANES
        + lax.broadcasted_iota(jnp.int32, accum.shape, 1)
    )
    sums = accum[...]
    for i in range(slots):
        new_table[pl.ds(picked[i], 1), :] = (
            table[pl.ds(picked[i], 1), :] - change[i : i + 1, :]
        )
        sums = jnp.where(flat == picked[i], new[i : i + 1, :], sums)
    new_accum[...] = sums


def per_device(
    user_feats, tower_weight, table, accum, neg_ids, negative_counts, negative_log_prob, pos_slot
):
    shape = jax.ShapeDtypeStruct
    plane, square = ("x", "y", "core"), ("x", "y")
    smem, hbm = spec(pltpu.SMEM), spec(pltpu.HBM)
    dma = pltpu.SemaphoreType.DMA
    slots = NARROW * PART
    swap = [(0, 1), (1, 0)]
    picked = pl.pallas_call(
        pick_kernel,
        name="pick_rows",
        out_shape=shape((Z, 16, LANES), BF16),
        in_specs=[smem, smem, spec(), hbm],
        out_specs=spec(),
        scratch_shapes=[
            pltpu.VMEM((PART, 8, 2 * LANES), F32),
            pltpu.VMEM((16, LANES), F32),
            dma((PART,)),
        ],
        compiler_params=params(60),
    )(neg_ids, negative_counts, negative_log_prob.reshape(1, -1), table)
    picked = lax.all_to_all(picked, "z", 0, 0, tiled=True)
    spread = pl.pallas_call(
        spread_kernel,
        name="spread_rows",
        out_shape=shape((SQUARE, 2 * ROWS + 16, LANES), BF16),
        in_specs=[spec()],
        out_specs=spec(),
        scratch_shapes=[pltpu.VMEM((2 * ROWS + 16, LANES), F32)],
        compiler_params=params(),
    )(picked)
    mine = lax.all_to_all(spread, square, 0, 0, tiled=True)
    queries = user_feats.shape[0]
    half_slots = SQUARE * ROWS
    feats2 = lax.ppermute(user_feats, "core", swap)
    query = pl.pallas_call(
        query_kernel,
        name="queries",
        out_shape=shape((2 * queries, 2 * LANES), BF16),
        in_specs=[spec()] * 3,
        out_specs=spec(),
        compiler_params=params(),
        cost_estimate=pl.CostEstimate(
            flops=16 * queries * LANES * 4 * LANES, bytes_accessed=2**20, transcendentals=0
        ),
    )(user_feats, feats2, tower_weight)
    expo, columns, stats = pl.pallas_call(
        score_kernel,
        name="scores",
        out_shape=(
            shape((2 * queries, half_slots), F32),
            shape((2 * queries, LANES), F32),
            shape((16, LANES), F32),
        ),
        in_specs=[spec()] * 3,
        out_specs=(spec(),) * 3,
        compiler_params=params(32),
    )(query, pos_slot.reshape(-1, LANES), mine)
    stats = lax.all_gather(stats, "core", axis=0)
    tower_part = (SQUARE, 32, LANES)
    dscore, kept, sent = pl.pallas_call(
        tower_kernel,
        name="tower_gradient",
        out_shape=(
            shape((2 * queries, half_slots), BF16),
            shape(tower_part, F32),
            shape(tower_part, BF16),
        ),
        in_specs=[spec()] * 6,
        out_specs=(spec(),) * 3,
        compiler_params=params(32),
    )(user_feats, feats2, mine, expo, columns, stats)
    got = lax.all_gather(sent, "core", axis=0)
    slot_part = pl.pallas_call(
        slot_kernel,
        name="slot_gradient",
        out_shape=shape((SQUARE, 2 * ROWS, LANES), BF16),
        in_specs=[spec()] * 2,
        out_specs=spec(),
        compiler_params=params(32),
        cost_estimate=pl.CostEstimate(
            flops=8 * queries * half_slots * LANES, bytes_accessed=2**21, transcendentals=0
        ),
    )(dscore, query)
    chip = pl.pallas_call(
        join_kernel,
        name="join_tower",
        out_shape=shape((SQUARE, 2 * ROWS + 32, LANES), BF16),
        in_specs=[spec()] * 3,
        out_specs=spec(),
        compiler_params=params(),
    )(slot_part, kept, got)
    chip = lax.all_to_all(chip, square, 0, 0, tiled=True)
    sums = pl.pallas_call(
        plane_sum_kernel,
        name="plane_sum",
        out_shape=shape((Z, 40, LANES), BF16),
        in_specs=[spec()],
        out_specs=spec(),
        scratch_shapes=[pltpu.VMEM((Z, 40, LANES), F32)],
        compiler_params=params(),
    )(chip)
    sums = lax.all_to_all(sums, "z", 0, 0, tiled=True)
    whole = pl.pallas_call(
        z_sum_kernel,
        name="z_sum",
        out_shape=shape((PEERS, 40, LANES), BF16),
        in_specs=[spec()],
        out_specs=spec(),
        compiler_params=params(),
    )(sums)
    whole = lax.all_to_all(whole, plane, 0, 0, tiled=True)
    new_table, new_accum, tower_grad = pl.pallas_call(
        update_kernel,
        name="row_update",
        out_shape=(
            shape(table.shape, F32),
            shape((8, LANES), F32),
            shape(tower_weight.shape, F32),
        ),
        in_specs=[smem, smem, spec(), spec(), spec()],
        out_specs=(spec(), spec(), spec()),
        scratch_shapes=[pltpu.VMEM((slots, 2 * LANES), F32)],
        compiler_params=params(),
    )(neg_ids, accum, whole, table, accum.reshape(8, LANES))
    return (new_table, new_accum.reshape(-1), tower_grad)


def solution(mesh):
    fine = Mesh(mesh.devices.reshape(X, Z, Y, CORE), ("x", "z", "y", "core"))
    wide, narrow = ("x", "z"), ("y", "core")
    return jax.shard_map(
        per_device,
        mesh=fine,
        in_specs=(
            P(wide + narrow, None),
            P(),
            P(wide, None),
            P(wide),
            P(wide),
            P(wide),
            P(wide),
            P(wide + narrow),
        ),
        out_specs=(P(wide, None), P(wide), P()),
        check_vma=False,
    )
```

```python
import jax
import jax.numpy as jnp
from jax import lax
from jax.experimental import pallas as pl
from jax.experimental.pallas import tpu as pltpu
from jax.sharding import Mesh, PartitionSpec as P

LEARN_RATE = 0.05
X, Z, YH, YL, CORE = 4, 16, 2, 2, 2
Y = YH * YL
NARROW = Y * CORE
PEERS = X * NARROW
SQUARE = X * Y
PART = 4
LANES = 128
ROWS = PART * Z
STEP = 4
PACK = 2 * ROWS + 16
F32, BF16 = jnp.float32, jnp.bfloat16


def spec(space=pltpu.VMEM):
    return pl.BlockSpec(memory_space=space)


def params(mib=16):
    return pltpu.CompilerParams(vmem_limit_bytes=mib * 1024 * 1024)


def pick_kernel(ids, counts, log_prob, table, out, groups, tile, sems):
    z, yl, core = lax.axis_index("z"), lax.axis_index("yl"), lax.axis_index("core")
    firsts = [((yh * YL + yl) * CORE + core) * PART for yh in range(YH)]
    rows = [lax.rem(ids[first + i], table.shape[0]) for first in firsts for i in range(PART)]
    copies = []
    for i, row in enumerate(rows):
        start = pl.multiple_of((row >> 3) << 3, 8)
        copies.append(
            pltpu.make_async_copy(table.at[pl.ds(start, 8), :], groups.at[i], sems.at[i])
        )
        copies[-1].start()
    own = log_prob.shape[1]
    lane = lax.broadcasted_iota(jnp.int32, (8, LANES), 1)
    row_at = lax.broadcasted_iota(jnp.int32, (8, LANES), 0)
    value = jnp.concatenate(
        [log_prob[...].astype(F32), jnp.zeros((1, LANES - own), F32)], axis=1
    )
    value = jnp.broadcast_to(value, (8, LANES))
    value = jnp.where(lane < counts[0], value, 1e30)
    shifts = jnp.zeros((8, LANES), F32)
    for yh, first in enumerate(firsts):
        part = jnp.where((lane >= first) & (lane < first + PART), value, 0.0)
        target = yl * ROWS + z * PART
        part = pltpu.roll(part, lax.rem(target - first + LANES, LANES), 1)
        shifts = jnp.where(row_at == yh, part, shifts)
    tile[YH * 8 :, :] = shifts
    for i, row in enumerate(rows):
        copies[i].wait()
        row = groups[i, pl.ds(row & 7, 1), :]
        at = (i // PART) * 8 + i % PART
        tile[at : at + 1, :] = row[:, 0:LANES]
        tile[at + PART : at + PART + 1, :] = row[:, LANES:]
    out[...] = jnp.broadcast_to(tile[...].astype(BF16)[None], out.shape)


def spread_kernel(got, out, tile):
    value = got[...].astype(F32)
    shifts = jnp.sum(value[:, YH * 8 :], axis=0)
    row_at = lax.broadcasted_iota(jnp.int32, (8, LANES), 0)
    for yh in range(YH):
        base = yh * PACK
        for z in range(Z):
            at = base + z * PART
            tile[at : at + PART, :] = value[z, yh * 8 : yh * 8 + PART]
            tile[at + ROWS : at + ROWS + PART, :] = value[z, yh * 8 + PART : yh * 8 + 8]
        base = base + 2 * ROWS
        tile[base : base + 8, :] = jnp.where(row_at == 0, shifts[yh : yh + 1], 0.0)
        tile[base + 8 : base + 16, :] = jnp.zeros((8, LANES), F32)
    out[...] = jnp.broadcast_to(tile[...].astype(BF16)[None], out.shape)


def chunk(got, at, start, stop):
    x, yh, yl = at // Y, at // YL % YH, at % YL
    return got[x * YL + yl, yh * PACK + start : yh * PACK + stop, :]


def cand_block(got, first, count):
    chips = range(first, first + count)
    left = jnp.concatenate([chunk(got, at, 0, ROWS) for at in chips], axis=0)
    right = jnp.concatenate([chunk(got, at, ROWS, 2 * ROWS) for at in chips], axis=0)
    return jnp.concatenate([left, right], axis=1)


def query_kernel(feats, feats2, weight, query):
    queries = feats.shape[0]
    query[0:queries, :] = jnp.dot(
        feats[...], weight[...], preferred_element_type=F32
    ).astype(BF16)
    query[queries:, :] = jnp.dot(
        feats2[...], weight[...], preferred_element_type=F32
    ).astype(BF16)


def score_kernel(query, pos, got, expo, columns, stats):
    blocks = query.shape[0] // LANES
    block = STEP * ROWS
    top = None
    for t in range(SQUARE // STEP):
        first = t * STEP
        value = lax.dot_general(
            query[...],
            cand_block(got, first, STEP),
            (((1,), (1,)), ((), ())),
            preferred_element_type=F32,
        )
        shifts = [
            chunk(got, first + i, 2 * ROWS, PACK).astype(F32)[0:1, :] for i in range(STEP)
        ]
        row = jnp.concatenate(
            [shifts[i] + shifts[i + 1] for i in range(0, STEP, 2)], axis=1
        )
        value = value * 2.0 - row
        expo[:, t * block : (t + 1) * block] = value
        part = value[:, 0:LANES]
        for i in range(1, block // LANES):
            part = jnp.maximum(part, value[:, i * LANES : (i + 1) * LANES])
        top = part if top is None else jnp.maximum(top, part)
    top = jnp.max(top, axis=1, keepdims=True)
    total = None
    for t in range(SQUARE // STEP):
        value = jnp.exp(expo[:, t * block : (t + 1) * block] - top)
        expo[:, t * block : (t + 1) * block] = value
        part = value[:, 0:LANES]
        for i in range(1, block // LANES):
            part = part + value[:, i * LANES : (i + 1) * LANES]
        total = part if total is None else total + part
    total = jnp.sum(total, axis=1, keepdims=True)
    lane = lax.broadcasted_iota(jnp.int32, (blocks * LANES, LANES), 1)
    both = jnp.where(lane == 0, top, total)
    columns[...] = both
    rows = [both[i * LANES : (i + 1) * LANES].T for i in range(blocks)]
    stats[0:blocks, :] = jnp.concatenate([row[0:1] for row in rows], axis=0)
    stats[blocks : 2 * blocks, :] = jnp.concatenate([row[1:2] for row in rows], axis=0)
    slot = pos[...]
    slot = (
        (((slot >> 2) & 1) << 10)
        + ((slot >> 9) << 8)
        + (((slot >> 3) & 3) << 6)
        + (((slot >> 5) & 15) << 2)
        + (slot & 3)
    ).astype(F32)
    pad = jnp.zeros((stats.shape[0] - 2 * blocks - slot.shape[0], LANES), F32)
    stats[2 * blocks :, :] = jnp.concatenate([slot, pad], axis=0)


def tower_kernel(feats, feats2, got, expo, columns, stats, dscore, kept, sent):
    queries = feats.shape[0]
    block = STEP * ROWS
    blocks = 2 * queries // LANES
    core = lax.axis_index("core")
    mine, theirs = stats[core], stats[1 - core]
    tiles = []
    for i in range(blocks):
        other = (i + blocks // 2) % blocks
        owner = mine if i < blocks // 2 else theirs
        at = 2 * blocks + i % (blocks // 2)
        tile = [
            theirs[other : other + 1],
            theirs[blocks + other : blocks + other + 1],
            owner[at : at + 1],
            jnp.zeros((5, LANES), F32),
        ]
        tiles.append(jnp.concatenate(tile, axis=0).T)
    tiles = jnp.concatenate(tiles, axis=0)
    top1, total1 = columns[:, 0:1], columns[:, 1:2]
    top2, total2, slot = tiles[:, 0:1], tiles[:, 1:2], tiles[:, 2:3]
    top = jnp.maximum(top1, top2)
    share = jnp.exp(top1 - top)
    scale = share / (total1 * share + total2 * jnp.exp(top2 - top))
    slot = slot.astype(jnp.int32) - core * (SQUARE * ROWS)
    lane = lax.broadcasted_iota(jnp.int32, (2 * queries, block), 1)
    for t in range(SQUARE // STEP):
        hit = jnp.where(lane == slot - t * block, 1.0, 0.0)
        dscore[:, t * block : (t + 1) * block] = (
            expo[:, t * block : (t + 1) * block] * scale - hit
        ).astype(BF16)
    dquery = jnp.dot(dscore[...], cand_block(got, 0, SQUARE), preferred_element_type=F32)
    dquery = (dquery * 2.0).astype(BF16)
    contract = (((0,), (0,)), ((), ()))
    tower = lax.dot_general(
        feats[...], dquery[0:queries], contract, preferred_element_type=F32
    ) + lax.dot_general(feats2[...], dquery[queries:], contract, preferred_element_type=F32)
    for half in range(2):
        part = tower[:, half * LANES : (half + 1) * LANES].reshape(SQUARE, CORE, 16, LANES)
        low, high = part[:, 0], part[:, 1]
        rows = slice(half * 16, half * 16 + 16)
        kept[:, rows, :] = jnp.where(core == 0, low, high)
        sent[:, rows, :] = jnp.where(core == 0, high, low).astype(BF16)


def slot_kernel(dscore, query, out):
    block = STEP * ROWS
    for t in range(SQUARE // STEP):
        grad = lax.dot_general(
            dscore[:, t * block : (t + 1) * block],
            query[...],
            (((0,), (0,)), ((), ())),
            preferred_element_type=F32,
        ).astype(BF16)
        for half in range(2):
            out[t * STEP : (t + 1) * STEP, half * ROWS : (half + 1) * ROWS, :] = grad[
                :, half * LANES : (half + 1) * LANES
            ].reshape(STEP, ROWS, LANES)


def join_kernel(slots, kept, got, out):
    theirs = got[1 - lax.axis_index("core")]
    out[:, 0 : 2 * ROWS, :] = slots[...]
    out[:, 2 * ROWS :, :] = (kept[...] + theirs.astype(F32)).astype(BF16)


def plane_sum_kernel(got, out, tile):
    total = got[0].astype(F32)
    for p in range(1, SQUARE):
        total = total + got[p].astype(F32)
    tower = total[2 * ROWS :]
    for z in range(Z):
        tile[z, 0:PART, :] = total[z * PART : (z + 1) * PART]
        tile[z, PART : 2 * PART, :] = total[ROWS + z * PART : ROWS + (z + 1) * PART]
        tile[z, 8:40, :] = tower
    out[...] = tile[...].astype(BF16)


def z_sum_kernel(got, out):
    total = got[0].astype(F32)
    for z in range(1, Z):
        total = total + got[z].astype(F32)
    out[...] = jnp.broadcast_to(total.astype(BF16)[None], out.shape)


def update_kernel(
    ids, accum_at, got, table, accum, new_table, new_accum, tower, grad
):
    rows = table.shape[0]
    value = got[...].astype(F32)
    tower[:, 0:LANES] = value[:, 8:24, :].reshape(PEERS * 16, LANES)
    tower[:, LANES:] = value[:, 24:40, :].reshape(PEERS * 16, LANES)
    own = lax.axis_index("x") * NARROW
    for n in range(NARROW):
        part = got[own + n].astype(F32)
        grad[n * PART : (n + 1) * PART, 0:LANES] = part[0:PART]
        grad[n * PART : (n + 1) * PART, LANES:] = part[PART : 2 * PART]
    slots = NARROW * PART
    row_grad = grad[...] * 2.0
    square = jnp.mean(row_grad * row_grad, axis=1, keepdims=True)
    at = lax.broadcasted_iota(jnp.int32, (slots, 1), 0)
    picked = [lax.rem(ids[i], rows) for i in range(slots)]
    old = jnp.zeros((slots, 1), F32)
    for i in range(slots):
        old = jnp.where(at == i, accum_at[picked[i]], old)
    new = old + square
    change = LEARN_RATE * row_grad / jnp.sqrt(new)
    new_table[...] = table[...]
    flat = (
        lax.broadcasted_iota(jnp.int32, accum.shape, 0) * LANES
        + lax.broadcasted_iota(jnp.int32, accum.shape, 1)
    )
    sums = accum[...]
    for i in range(slots):
        new_table[pl.ds(picked[i], 1), :] = (
            table[pl.ds(picked[i], 1), :] - change[i : i + 1, :]
        )
        sums = jnp.where(flat == picked[i], new[i : i + 1, :], sums)
    new_accum[...] = sums


def per_device(
    user_feats, tower_weight, table, accum, neg_ids, negative_counts, negative_log_prob, pos_slot
):
    shape = jax.ShapeDtypeStruct
    plane, square = ("x", "yh", "yl", "core"), ("x", "yh", "yl")
    smem, hbm = spec(pltpu.SMEM), spec(pltpu.HBM)
    dma = pltpu.SemaphoreType.DMA
    slots = NARROW * PART
    swap = [(0, 1), (1, 0)]
    picked = pl.pallas_call(
        pick_kernel,
        name="pick_rows",
        out_shape=shape((Z, YH * 8 + 8, LANES), BF16),
        in_specs=[smem, smem, spec(), hbm],
        out_specs=spec(),
        scratch_shapes=[
            pltpu.VMEM((YH * PART, 8, 2 * LANES), F32),
            pltpu.VMEM((YH * 8 + 8, LANES), F32),
            dma((YH * PART,)),
        ],
        compiler_params=params(60),
    )(neg_ids, negative_counts, negative_log_prob.reshape(1, -1), table)
    picked = lax.all_to_all(picked, "z", 0, 0, tiled=True)
    spread = pl.pallas_call(
        spread_kernel,
        name="spread_rows",
        out_shape=shape((X * YL, YH * PACK, LANES), BF16),
        in_specs=[spec()],
        out_specs=spec(),
        scratch_shapes=[pltpu.VMEM((YH * PACK, LANES), F32)],
        compiler_params=params(),
    )(picked)
    mine = lax.all_to_all(spread, ("x", "yl"), 0, 0, tiled=True)
    queries = user_feats.shape[0]
    half_slots = SQUARE * ROWS
    feats2 = lax.ppermute(user_feats, "core", swap)
    query = pl.pallas_call(
        query_kernel,
        name="queries",
        out_shape=shape((2 * queries, 2 * LANES), BF16),
        in_specs=[spec()] * 3,
        out_specs=spec(),
        compiler_params=params(),
        cost_estimate=pl.CostEstimate(
            flops=16 * queries * LANES * 4 * LANES, bytes_accessed=2**20, transcendentals=0
        ),
    )(user_feats, feats2, tower_weight)
    expo, columns, stats = pl.pallas_call(
        score_kernel,
        name="scores",
        out_shape=(
            shape((2 * queries, half_slots), F32),
            shape((2 * queries, LANES), F32),
            shape((16, LANES), F32),
        ),
        in_specs=[spec()] * 3,
        out_specs=(spec(),) * 3,
        compiler_params=params(32),
    )(query, pos_slot.reshape(-1, LANES), mine)
    stats = lax.all_gather(stats, "core", axis=0)
    tower_part = (SQUARE, 32, LANES)
    dscore, kept, sent = pl.pallas_call(
        tower_kernel,
        name="tower_gradient",
        out_shape=(
            shape((2 * queries, half_slots), BF16),
            shape(tower_part, F32),
            shape(tower_part, BF16),
        ),
        in_specs=[spec()] * 6,
        out_specs=(spec(),) * 3,
        compiler_params=params(32),
    )(user_feats, feats2, mine, expo, columns, stats)
    got = lax.all_gather(sent, "core", axis=0)
    slot_part = pl.pallas_call(
        slot_kernel,
        name="slot_gradient",
        out_shape=shape((SQUARE, 2 * ROWS, LANES), BF16),
        in_specs=[spec()] * 2,
        out_specs=spec(),
        compiler_params=params(32),
        cost_estimate=pl.CostEstimate(
            flops=8 * queries * half_slots * LANES, bytes_accessed=2**21, transcendentals=0
        ),
    )(dscore, query)
    chip = pl.pallas_call(
        join_kernel,
        name="join_tower",
        out_shape=shape((SQUARE, 2 * ROWS + 32, LANES), BF16),
        in_specs=[spec()] * 3,
        out_specs=spec(),
        compiler_params=params(),
    )(slot_part, kept, got)
    chip = lax.all_to_all(chip, square, 0, 0, tiled=True)
    sums = pl.pallas_call(
        plane_sum_kernel,
        name="plane_sum",
        out_shape=shape((Z, 40, LANES), BF16),
        in_specs=[spec()],
        out_specs=spec(),
        scratch_shapes=[pltpu.VMEM((Z, 40, LANES), F32)],
        compiler_params=params(),
    )(chip)
    sums = lax.all_to_all(sums, "z", 0, 0, tiled=True)
    whole = pl.pallas_call(
        z_sum_kernel,
        name="z_sum",
        out_shape=shape((PEERS, 40, LANES), BF16),
        in_specs=[spec()],
        out_specs=spec(),
        compiler_params=params(),
    )(sums)
    whole = lax.all_to_all(whole, plane, 0, 0, tiled=True)
    new_table, new_accum, tower_grad = pl.pallas_call(
        update_kernel,
        name="row_update",
        out_shape=(
            shape(table.shape, F32),
            shape((8, LANES), F32),
            shape(tower_weight.shape, F32),
        ),
        in_specs=[smem, smem, spec(), spec(), spec()],
        out_specs=(spec(), spec(), spec()),
        scratch_shapes=[pltpu.VMEM((slots, 2 * LANES), F32)],
        compiler_params=params(),
    )(neg_ids, accum, whole, table, accum.reshape(8, LANES))
    return (new_table, new_accum.reshape(-1), tower_grad)


def solution(mesh):
    fine = Mesh(mesh.devices.reshape(X, Z, YH, YL, CORE), ("x", "z", "yh", "yl", "core"))
    wide, narrow = ("x", "z"), ("yh", "yl", "core")
    return jax.shard_map(
        per_device,
        mesh=fine,
        in_specs=(
            P(wide + narrow, None),
            P(),
            P(wide, None),
            P(wide),
            P(wide),
            P(wide),
            P(wide),
            P(wide + narrow),
        ),
        out_specs=(P(wide, None), P(wide), P()),
        check_vma=False,
    )
```

```python
import jax
import jax.numpy as jnp
from jax import lax
from jax.experimental import pallas as pl
from jax.experimental.pallas import tpu as pltpu
from jax.sharding import Mesh, PartitionSpec as P

LEARN_RATE = 0.05
X, Z, YH, YL, CORE = 4, 16, 2, 2, 2
Y = YH * YL
NARROW = Y * CORE
PEERS = X * NARROW
SQUARE = X * Y
PART = 4
LANES = 128
ROWS = PART * Z
STEP = 4
PACK = 2 * ROWS + 16
F32, BF16 = jnp.float32, jnp.bfloat16


def spec(space=pltpu.VMEM):
    return pl.BlockSpec(memory_space=space)


def params(mib=16):
    return pltpu.CompilerParams(vmem_limit_bytes=mib * 1024 * 1024)


def pick_kernel(ids, counts, log_prob, table, out, groups, tile, sems):
    z, yl, core = lax.axis_index("z"), lax.axis_index("yl"), lax.axis_index("core")
    firsts = [((yh * YL + yl) * CORE + core) * PART for yh in range(YH)]
    rows = [lax.rem(ids[first + i], table.shape[0]) for first in firsts for i in range(PART)]
    copies = []
    for i, row in enumerate(rows):
        start = pl.multiple_of((row >> 3) << 3, 8)
        copies.append(
            pltpu.make_async_copy(table.at[pl.ds(start, 8), :], groups.at[i], sems.at[i])
        )
        copies[-1].start()
    own = log_prob.shape[1]
    lane = lax.broadcasted_iota(jnp.int32, (8, LANES), 1)
    row_at = lax.broadcasted_iota(jnp.int32, (8, LANES), 0)
    value = jnp.concatenate(
        [log_prob[...].astype(F32), jnp.zeros((1, LANES - own), F32)], axis=1
    )
    value = jnp.broadcast_to(value, (8, LANES))
    value = jnp.where(lane < counts[0], value, 1e30)
    shifts = jnp.zeros((8, LANES), F32)
    for yh, first in enumerate(firsts):
        part = jnp.where((lane >= first) & (lane < first + PART), value, 0.0)
        target = yl * ROWS + z * PART
        part = pltpu.roll(part, lax.rem(target - first + LANES, LANES), 1)
        shifts = jnp.where(row_at == yh, part, shifts)
    tile[YH * 8 :, :] = shifts
    for i, row in enumerate(rows):
        copies[i].wait()
        row = groups[i, pl.ds(row & 7, 1), :]
        at = (i // PART) * 8 + i % PART
        tile[at : at + 1, :] = row[:, 0:LANES]
        tile[at + PART : at + PART + 1, :] = row[:, LANES:]
    out[...] = jnp.broadcast_to(tile[...].astype(BF16)[None], out.shape)


def spread_kernel(got, out, tile):
    value = got[...].astype(F32)
    shifts = jnp.sum(value[:, YH * 8 :], axis=0)
    row_at = lax.broadcasted_iota(jnp.int32, (8, LANES), 0)
    for yh in range(YH):
        base = yh * PACK
        for z in range(Z):
            at = base + z * PART
            tile[at : at + PART, :] = value[z, yh * 8 : yh * 8 + PART]
            tile[at + ROWS : at + ROWS + PART, :] = value[z, yh * 8 + PART : yh * 8 + 8]
        base = base + 2 * ROWS
        tile[base : base + 8, :] = jnp.where(row_at == 0, shifts[yh : yh + 1], 0.0)
        tile[base + 8 : base + 16, :] = jnp.zeros((8, LANES), F32)
    out[...] = jnp.broadcast_to(tile[...].astype(BF16)[None], out.shape)


def chunk(got, at, start, stop):
    x, yh, yl = at // Y, at // YL % YH, at % YL
    return got[x * YL + yl, yh * PACK + start : yh * PACK + stop, :]


def cand_block(got, first, count):
    chips = range(first, first + count)
    left = jnp.concatenate([chunk(got, at, 0, ROWS) for at in chips], axis=0)
    right = jnp.concatenate([chunk(got, at, ROWS, 2 * ROWS) for at in chips], axis=0)
    return jnp.concatenate([left, right], axis=1)


def query_kernel(feats, both, weight, query):
    theirs = both[1 - lax.axis_index("core")]
    queries = feats.shape[0]
    query[0:queries, :] = jnp.dot(
        feats[...], weight[...], preferred_element_type=F32
    ).astype(BF16)
    query[queries:, :] = jnp.dot(
        theirs, weight[...], preferred_element_type=F32
    ).astype(BF16)


def score_kernel(query, pos, got, expo, columns, stats):
    blocks = query.shape[0] // LANES
    block = STEP * ROWS
    top = None
    for t in range(SQUARE // STEP):
        first = t * STEP
        value = lax.dot_general(
            query[...],
            cand_block(got, first, STEP),
            (((1,), (1,)), ((), ())),
            preferred_element_type=F32,
        )
        shifts = [
            chunk(got, first + i, 2 * ROWS, PACK).astype(F32)[0:1, :] for i in range(STEP)
        ]
        row = jnp.concatenate(
            [shifts[i] + shifts[i + 1] for i in range(0, STEP, 2)], axis=1
        )
        value = value * 2.0 - row
        expo[:, t * block : (t + 1) * block] = value
        part = value[:, 0:LANES]
        for i in range(1, block // LANES):
            part = jnp.maximum(part, value[:, i * LANES : (i + 1) * LANES])
        top = part if top is None else jnp.maximum(top, part)
    top = jnp.max(top, axis=1, keepdims=True)
    total = None
    for t in range(SQUARE // STEP):
        value = jnp.exp(expo[:, t * block : (t + 1) * block] - top)
        expo[:, t * block : (t + 1) * block] = value
        part = value[:, 0:LANES]
        for i in range(1, block // LANES):
            part = part + value[:, i * LANES : (i + 1) * LANES]
        total = part if total is None else total + part
    total = jnp.sum(total, axis=1, keepdims=True)
    lane = lax.broadcasted_iota(jnp.int32, (blocks * LANES, LANES), 1)
    both = jnp.where(lane == 0, top, total)
    columns[...] = both
    rows = [both[i * LANES : (i + 1) * LANES].T for i in range(blocks)]
    stats[0:blocks, :] = jnp.concatenate([row[0:1] for row in rows], axis=0)
    stats[blocks : 2 * blocks, :] = jnp.concatenate([row[1:2] for row in rows], axis=0)
    slot = pos[...]
    slot = (
        (((slot >> 2) & 1) << 10)
        + ((slot >> 9) << 8)
        + (((slot >> 3) & 3) << 6)
        + (((slot >> 5) & 15) << 2)
        + (slot & 3)
    ).astype(F32)
    pad = jnp.zeros((stats.shape[0] - 2 * blocks - slot.shape[0], LANES), F32)
    stats[2 * blocks :, :] = jnp.concatenate([slot, pad], axis=0)


def tower_kernel(feats, both, got, expo, columns, stats, dscore, kept, sent):
    queries = feats.shape[0]
    block = STEP * ROWS
    blocks = 2 * queries // LANES
    core = lax.axis_index("core")
    mine, theirs = stats[core], stats[1 - core]
    tiles = []
    for i in range(blocks):
        other = (i + blocks // 2) % blocks
        owner = mine if i < blocks // 2 else theirs
        at = 2 * blocks + i % (blocks // 2)
        tile = [
            theirs[other : other + 1],
            theirs[blocks + other : blocks + other + 1],
            owner[at : at + 1],
            jnp.zeros((5, LANES), F32),
        ]
        tiles.append(jnp.concatenate(tile, axis=0).T)
    tiles = jnp.concatenate(tiles, axis=0)
    top1, total1 = columns[:, 0:1], columns[:, 1:2]
    top2, total2, slot = tiles[:, 0:1], tiles[:, 1:2], tiles[:, 2:3]
    top = jnp.maximum(top1, top2)
    share = jnp.exp(top1 - top)
    scale = share / (total1 * share + total2 * jnp.exp(top2 - top))
    slot = slot.astype(jnp.int32) - core * (SQUARE * ROWS)
    lane = lax.broadcasted_iota(jnp.int32, (2 * queries, block), 1)
    for t in range(SQUARE // STEP):
        hit = jnp.where(lane == slot - t * block, 1.0, 0.0)
        dscore[:, t * block : (t + 1) * block] = (
            expo[:, t * block : (t + 1) * block] * scale - hit
        ).astype(BF16)
    dquery = jnp.dot(dscore[...], cand_block(got, 0, SQUARE), preferred_element_type=F32)
    dquery = (dquery * 2.0).astype(BF16)
    contract = (((0,), (0,)), ((), ()))
    tower = lax.dot_general(
        feats[...], dquery[0:queries], contract, preferred_element_type=F32
    ) + lax.dot_general(both[1 - core], dquery[queries:], contract, preferred_element_type=F32)
    for half in range(2):
        part = tower[:, half * LANES : (half + 1) * LANES].reshape(SQUARE, CORE, 16, LANES)
        low, high = part[:, 0], part[:, 1]
        rows = slice(half * 16, half * 16 + 16)
        kept[:, rows, :] = jnp.where(core == 0, low, high)
        sent[:, rows, :] = jnp.where(core == 0, high, low).astype(BF16)


def slot_kernel(dscore, query, out):
    block = STEP * ROWS
    for t in range(SQUARE // STEP):
        grad = lax.dot_general(
            dscore[:, t * block : (t + 1) * block],
            query[...],
            (((0,), (0,)), ((), ())),
            preferred_element_type=F32,
        ).astype(BF16)
        for half in range(2):
            out[t * STEP : (t + 1) * STEP, half * ROWS : (half + 1) * ROWS, :] = grad[
                :, half * LANES : (half + 1) * LANES
            ].reshape(STEP, ROWS, LANES)


def join_kernel(slots, kept, got, out):
    theirs = got[1 - lax.axis_index("core")]
    out[:, 0 : 2 * ROWS, :] = slots[...]
    out[:, 2 * ROWS :, :] = (kept[...] + theirs.astype(F32)).astype(BF16)


def plane_sum_kernel(got, out, tile):
    total = got[0].astype(F32)
    for p in range(1, SQUARE):
        total = total + got[p].astype(F32)
    tower = total[2 * ROWS :]
    for z in range(Z):
        tile[z, 0:PART, :] = total[z * PART : (z + 1) * PART]
        tile[z, PART : 2 * PART, :] = total[ROWS + z * PART : ROWS + (z + 1) * PART]
        tile[z, 8:40, :] = tower
    out[...] = tile[...].astype(BF16)


def z_sum_kernel(got, out):
    total = got[0].astype(F32)
    for z in range(1, Z):
        total = total + got[z].astype(F32)
    out[...] = jnp.broadcast_to(total.astype(BF16)[None], out.shape)


def update_kernel(
    ids, accum_at, got, table, accum, new_table, new_accum, tower, grad
):
    rows = table.shape[0]
    value = got[...].astype(F32)
    tower[:, 0:LANES] = value[:, 8:24, :].reshape(PEERS * 16, LANES)
    tower[:, LANES:] = value[:, 24:40, :].reshape(PEERS * 16, LANES)
    own = lax.axis_index("x") * NARROW
    for n in range(NARROW):
        part = got[own + n].astype(F32)
        grad[n * PART : (n + 1) * PART, 0:LANES] = part[0:PART]
        grad[n * PART : (n + 1) * PART, LANES:] = part[PART : 2 * PART]
    slots = NARROW * PART
    row_grad = grad[...] * 2.0
    square = jnp.mean(row_grad * row_grad, axis=1, keepdims=True)
    at = lax.broadcasted_iota(jnp.int32, (slots, 1), 0)
    picked = [lax.rem(ids[i], rows) for i in range(slots)]
    old = jnp.zeros((slots, 1), F32)
    for i in range(slots):
        old = jnp.where(at == i, accum_at[picked[i]], old)
    new = old + square
    change = LEARN_RATE * row_grad / jnp.sqrt(new)
    new_table[...] = table[...]
    flat = (
        lax.broadcasted_iota(jnp.int32, accum.shape, 0) * LANES
        + lax.broadcasted_iota(jnp.int32, accum.shape, 1)
    )
    sums = accum[...]
    for i in range(slots):
        new_table[pl.ds(picked[i], 1), :] = (
            table[pl.ds(picked[i], 1), :] - change[i : i + 1, :]
        )
        sums = jnp.where(flat == picked[i], new[i : i + 1, :], sums)
    new_accum[...] = sums


def per_device(
    user_feats, tower_weight, table, accum, neg_ids, negative_counts, negative_log_prob, pos_slot
):
    shape = jax.ShapeDtypeStruct
    plane, square = ("x", "yh", "yl", "core"), ("x", "yh", "yl")
    smem, hbm = spec(pltpu.SMEM), spec(pltpu.HBM)
    dma = pltpu.SemaphoreType.DMA
    slots = NARROW * PART
    picked = pl.pallas_call(
        pick_kernel,
        name="pick_rows",
        out_shape=shape((Z, YH * 8 + 8, LANES), BF16),
        in_specs=[smem, smem, spec(), hbm],
        out_specs=spec(),
        scratch_shapes=[
            pltpu.VMEM((YH * PART, 8, 2 * LANES), F32),
            pltpu.VMEM((YH * 8 + 8, LANES), F32),
            dma((YH * PART,)),
        ],
        compiler_params=params(60),
    )(neg_ids, negative_counts, negative_log_prob.reshape(1, -1), table)
    picked = lax.all_to_all(picked, "z", 0, 0, tiled=True)
    spread = pl.pallas_call(
        spread_kernel,
        name="spread_rows",
        out_shape=shape((X * YL, YH * PACK, LANES), BF16),
        in_specs=[spec()],
        out_specs=spec(),
        scratch_shapes=[pltpu.VMEM((YH * PACK, LANES), F32)],
        compiler_params=params(),
    )(picked)
    mine = lax.all_to_all(spread, ("x", "yl"), 0, 0, tiled=True)
    queries = user_feats.shape[0]
    half_slots = SQUARE * ROWS
    both = lax.all_gather(user_feats, "core", axis=0)
    query = pl.pallas_call(
        query_kernel,
        name="queries",
        out_shape=shape((2 * queries, 2 * LANES), BF16),
        in_specs=[spec()] * 3,
        out_specs=spec(),
        compiler_params=params(),
        cost_estimate=pl.CostEstimate(
            flops=16 * queries * LANES * 4 * LANES, bytes_accessed=2**20, transcendentals=0
        ),
    )(user_feats, both, tower_weight)
    expo, columns, stats = pl.pallas_call(
        score_kernel,
        name="scores",
        out_shape=(
            shape((2 * queries, half_slots), F32),
            shape((2 * queries, LANES), F32),
            shape((16, LANES), F32),
        ),
        in_specs=[spec()] * 3,
        out_specs=(spec(),) * 3,
        compiler_params=params(32),
    )(query, pos_slot.reshape(-1, LANES), mine)
    stats = lax.all_gather(stats, "core", axis=0)
    tower_part = (SQUARE, 32, LANES)
    dscore, kept, sent = pl.pallas_call(
        tower_kernel,
        name="tower_gradient",
        out_shape=(
            shape((2 * queries, half_slots), BF16),
            shape(tower_part, F32),
            shape(tower_part, BF16),
        ),
        in_specs=[spec()] * 6,
        out_specs=(spec(),) * 3,
        compiler_params=params(32),
    )(user_feats, both, mine, expo, columns, stats)
    got = lax.all_gather(sent, "core", axis=0)
    slot_part = pl.pallas_call(
        slot_kernel,
        name="slot_gradient",
        out_shape=shape((SQUARE, 2 * ROWS, LANES), BF16),
        in_specs=[spec()] * 2,
        out_specs=spec(),
        compiler_params=params(32),
        cost_estimate=pl.CostEstimate(
            flops=8 * queries * half_slots * LANES, bytes_accessed=2**21, transcendentals=0
        ),
    )(dscore, query)
    chip = pl.pallas_call(
        join_kernel,
        name="join_tower",
        out_shape=shape((SQUARE, 2 * ROWS + 32, LANES), BF16),
        in_specs=[spec()] * 3,
        out_specs=spec(),
        compiler_params=params(),
    )(slot_part, kept, got)
    chip = lax.all_to_all(chip, square, 0, 0, tiled=True)
    sums = pl.pallas_call(
        plane_sum_kernel,
        name="plane_sum",
        out_shape=shape((Z, 40, LANES), BF16),
        in_specs=[spec()],
        out_specs=spec(),
        scratch_shapes=[pltpu.VMEM((Z, 40, LANES), F32)],
        compiler_params=params(),
    )(chip)
    sums = lax.all_to_all(sums, "z", 0, 0, tiled=True)
    whole = pl.pallas_call(
        z_sum_kernel,
        name="z_sum",
        out_shape=shape((PEERS, 40, LANES), BF16),
        in_specs=[spec()],
        out_specs=spec(),
        compiler_params=params(),
    )(sums)
    whole = lax.all_to_all(whole, plane, 0, 0, tiled=True)
    new_table, new_accum, tower_grad = pl.pallas_call(
        update_kernel,
        name="row_update",
        out_shape=(
            shape(table.shape, F32),
            shape((8, LANES), F32),
            shape(tower_weight.shape, F32),
        ),
        in_specs=[smem, smem, spec(), spec(), spec()],
        out_specs=(spec(), spec(), spec()),
        scratch_shapes=[pltpu.VMEM((slots, 2 * LANES), F32)],
        compiler_params=params(),
    )(neg_ids, accum, whole, table, accum.reshape(8, LANES))
    return (new_table, new_accum.reshape(-1), tower_grad)


def solution(mesh):
    fine = Mesh(mesh.devices.reshape(X, Z, YH, YL, CORE), ("x", "z", "yh", "yl", "core"))
    wide, narrow = ("x", "z"), ("yh", "yl", "core")
    return jax.shard_map(
        per_device,
        mesh=fine,
        in_specs=(
            P(wide + narrow, None),
            P(),
            P(wide, None),
            P(wide),
            P(wide),
            P(wide),
            P(wide),
            P(wide + narrow),
        ),
        out_specs=(P(wide, None), P(wide), P()),
        check_vma=False,
    )
```

```python
import jax
import jax.numpy as jnp
from jax import lax
from jax.experimental import pallas as pl
from jax.experimental.pallas import tpu as pltpu
from jax.sharding import Mesh, PartitionSpec as P

LEARN_RATE = 0.05
X, Z, YH, YL, CORE = 4, 16, 2, 2, 2
Y = YH * YL
NARROW = Y * CORE
PEERS = X * NARROW
SQUARE = X * Y
PART = 4
LANES = 128
ROWS = PART * Z
STEP = 4
PACK = 2 * ROWS + 16
F32, BF16 = jnp.float32, jnp.bfloat16


def spec(space=pltpu.VMEM):
    return pl.BlockSpec(memory_space=space)


def params(mib=16):
    return pltpu.CompilerParams(vmem_limit_bytes=mib * 1024 * 1024)


def pick_kernel(ids, counts, log_prob, table, out, groups, tile, sems):
    z, yl, core = lax.axis_index("z"), lax.axis_index("yl"), lax.axis_index("core")
    firsts = [((yh * YL + yl) * CORE + core) * PART for yh in range(YH)]
    rows = [lax.rem(ids[first + i], table.shape[0]) for first in firsts for i in range(PART)]
    copies = []
    for i, row in enumerate(rows):
        start = pl.multiple_of((row >> 3) << 3, 8)
        copies.append(
            pltpu.make_async_copy(table.at[pl.ds(start, 8), :], groups.at[i], sems.at[i])
        )
        copies[-1].start()
    own = log_prob.shape[1]
    lane = lax.broadcasted_iota(jnp.int32, (8, LANES), 1)
    row_at = lax.broadcasted_iota(jnp.int32, (8, LANES), 0)
    value = jnp.concatenate(
        [log_prob[...].astype(F32), jnp.zeros((1, LANES - own), F32)], axis=1
    )
    value = jnp.broadcast_to(value, (8, LANES))
    value = jnp.where(lane < counts[0], value, 1e30)
    shifts = jnp.zeros((8, LANES), F32)
    for yh, first in enumerate(firsts):
        part = jnp.where((lane >= first) & (lane < first + PART), value, 0.0)
        target = yl * ROWS + z * PART
        part = pltpu.roll(part, lax.rem(target - first + LANES, LANES), 1)
        shifts = jnp.where(row_at == yh, part, shifts)
    tile[YH * 8 :, :] = shifts
    for i, row in enumerate(rows):
        copies[i].wait()
        row = groups[i, pl.ds(row & 7, 1), :]
        at = (i // PART) * 8 + i % PART
        tile[at : at + 1, :] = row[:, 0:LANES]
        tile[at + PART : at + PART + 1, :] = row[:, LANES:]
    out[...] = jnp.broadcast_to(tile[...].astype(BF16)[None], out.shape)


def spread_kernel(got, out, tile):
    value = got[...].astype(F32)
    shifts = jnp.sum(value[:, YH * 8 :], axis=0)
    row_at = lax.broadcasted_iota(jnp.int32, (8, LANES), 0)
    for yh in range(YH):
        base = yh * PACK
        for z in range(Z):
            at = base + z * PART
            tile[at : at + PART, :] = value[z, yh * 8 : yh * 8 + PART]
            tile[at + ROWS : at + ROWS + PART, :] = value[z, yh * 8 + PART : yh * 8 + 8]
        base = base + 2 * ROWS
        tile[base : base + 8, :] = jnp.where(row_at == 0, shifts[yh : yh + 1], 0.0)
        tile[base + 8 : base + 16, :] = jnp.zeros((8, LANES), F32)
    out[...] = jnp.broadcast_to(tile[...].astype(BF16)[None], out.shape)


def chunk(got, at, start, stop):
    x, yh, yl = at // Y, at // YL % YH, at % YL
    return got[x * YL + yl, yh * PACK + start : yh * PACK + stop, :]


def cand_block(got, first, count):
    chips = range(first, first + count)
    left = jnp.concatenate([chunk(got, at, 0, ROWS) for at in chips], axis=0)
    right = jnp.concatenate([chunk(got, at, ROWS, 2 * ROWS) for at in chips], axis=0)
    return jnp.concatenate([left, right], axis=1)


def query_kernel(feats, feats2, weight, query):
    queries = feats.shape[0]
    query[0:queries, :] = jnp.dot(
        feats[...], weight[...], preferred_element_type=F32
    ).astype(BF16)
    query[queries:, :] = jnp.dot(
        feats2[...], weight[...], preferred_element_type=F32
    ).astype(BF16)


def score_kernel(query, pos, got, expo, columns, stats):
    blocks = query.shape[0] // LANES
    block = STEP * ROWS
    top = None
    for t in range(SQUARE // STEP):
        first = t * STEP
        value = lax.dot_general(
            query[...],
            cand_block(got, first, STEP),
            (((1,), (1,)), ((), ())),
            preferred_element_type=F32,
        )
        shifts = [
            chunk(got, first + i, 2 * ROWS, PACK).astype(F32)[0:1, :] for i in range(STEP)
        ]
        row = jnp.concatenate(
            [shifts[i] + shifts[i + 1] for i in range(0, STEP, 2)], axis=1
        )
        value = value * 2.0 - row
        expo[:, t * block : (t + 1) * block] = value
        part = value[:, 0:LANES]
        for i in range(1, block // LANES):
            part = jnp.maximum(part, value[:, i * LANES : (i + 1) * LANES])
        top = part if top is None else jnp.maximum(top, part)
    top = jnp.max(top, axis=1, keepdims=True)
    total = None
    for t in range(SQUARE // STEP):
        value = jnp.exp(expo[:, t * block : (t + 1) * block] - top)
        expo[:, t * block : (t + 1) * block] = value
        part = value[:, 0:LANES]
        for i in range(1, block // LANES):
            part = part + value[:, i * LANES : (i + 1) * LANES]
        total = part if total is None else total + part
    total = jnp.sum(total, axis=1, keepdims=True)
    lane = lax.broadcasted_iota(jnp.int32, (blocks * LANES, LANES), 1)
    both = jnp.where(lane == 0, top, total)
    columns[...] = both
    rows = [both[i * LANES : (i + 1) * LANES].T for i in range(blocks)]
    stats[0:blocks, :] = jnp.concatenate([row[0:1] for row in rows], axis=0)
    stats[blocks : 2 * blocks, :] = jnp.concatenate([row[1:2] for row in rows], axis=0)
    slot = pos[...]
    slot = (
        (((slot >> 2) & 1) << 10)
        + ((slot >> 9) << 8)
        + (((slot >> 3) & 3) << 6)
        + (((slot >> 5) & 15) << 2)
        + (slot & 3)
    ).astype(F32)
    pad = jnp.zeros((stats.shape[0] - 2 * blocks - slot.shape[0], LANES), F32)
    stats[2 * blocks :, :] = jnp.concatenate([slot, pad], axis=0)


def tower_kernel(feats, feats2, got, expo, columns, stats, dscore, kept, sent):
    queries = feats.shape[0]
    block = STEP * ROWS
    blocks = 2 * queries // LANES
    core = lax.axis_index("core")
    mine, theirs = stats[core], stats[1 - core]
    tiles = []
    for i in range(blocks):
        other = (i + blocks // 2) % blocks
        owner = mine if i < blocks // 2 else theirs
        at = 2 * blocks + i % (blocks // 2)
        tile = [
            theirs[other : other + 1],
            theirs[blocks + other : blocks + other + 1],
            owner[at : at + 1],
            jnp.zeros((5, LANES), F32),
        ]
        tiles.append(jnp.concatenate(tile, axis=0).T)
    tiles = jnp.concatenate(tiles, axis=0)
    top1, total1 = columns[:, 0:1], columns[:, 1:2]
    top2, total2, slot = tiles[:, 0:1], tiles[:, 1:2], tiles[:, 2:3]
    top = jnp.maximum(top1, top2)
    share = jnp.exp(top1 - top)
    scale = share / (total1 * share + total2 * jnp.exp(top2 - top))
    slot = slot.astype(jnp.int32) - core * (SQUARE * ROWS)
    lane = lax.broadcasted_iota(jnp.int32, (2 * queries, block), 1)
    for t in range(SQUARE // STEP):
        hit = jnp.where(lane == slot - t * block, 1.0, 0.0)
        dscore[:, t * block : (t + 1) * block] = (
            expo[:, t * block : (t + 1) * block] * scale - hit
        ).astype(BF16)
    dquery = jnp.dot(dscore[...], cand_block(got, 0, SQUARE), preferred_element_type=F32)
    dquery = (dquery * 2.0).astype(BF16)
    contract = (((0,), (0,)), ((), ()))
    tower = lax.dot_general(
        feats[...], dquery[0:queries], contract, preferred_element_type=F32
    ) + lax.dot_general(feats2[...], dquery[queries:], contract, preferred_element_type=F32)
    for half in range(2):
        part = tower[:, half * LANES : (half + 1) * LANES].reshape(SQUARE, CORE, 16, LANES)
        low, high = part[:, 0], part[:, 1]
        rows = slice(half * 16, half * 16 + 16)
        kept[:, rows, :] = jnp.where(core == 0, low, high)
        sent[:, rows, :] = jnp.where(core == 0, high, low).astype(BF16)


def slot_kernel(dscore, query, out):
    block = STEP * ROWS
    for t in range(SQUARE // STEP):
        grad = lax.dot_general(
            dscore[:, t * block : (t + 1) * block],
            query[...],
            (((0,), (0,)), ((), ())),
            preferred_element_type=F32,
        ).astype(BF16)
        for half in range(2):
            out[t * STEP : (t + 1) * STEP, half * ROWS : (half + 1) * ROWS, :] = grad[
                :, half * LANES : (half + 1) * LANES
            ].reshape(STEP, ROWS, LANES)


def join_kernel(slots, kept, got, out):
    theirs = got[1 - lax.axis_index("core")]
    out[:, 0 : 2 * ROWS, :] = slots[...]
    out[:, 2 * ROWS :, :] = (kept[...] + theirs.astype(F32)).astype(BF16)


def plane_sum_kernel(got, out, tile):
    total = got[0].astype(F32)
    for p in range(1, SQUARE):
        total = total + got[p].astype(F32)
    tower = total[2 * ROWS :]
    for z in range(Z):
        tile[z, 0:PART, :] = total[z * PART : (z + 1) * PART]
        tile[z, PART : 2 * PART, :] = total[ROWS + z * PART : ROWS + (z + 1) * PART]
        tile[z, 8:40, :] = tower
    out[...] = tile[...].astype(BF16)


def z_sum_kernel(got, out):
    total = got[0].astype(F32)
    for z in range(1, Z):
        total = total + got[z].astype(F32)
    out[...] = jnp.broadcast_to(total.astype(BF16)[None], out.shape)


def update_kernel(
    ids, accum_at, got, table, accum, new_table, new_accum, tower, grad
):
    rows = table.shape[0]
    value = got[...].astype(F32)
    left = jnp.stack([value[core, :, 8:24, :] for core in range(CORE)], axis=1)
    right = jnp.stack([value[core, :, 24:40, :] for core in range(CORE)], axis=1)
    tower[:, 0:LANES] = left.reshape(PEERS * 16, LANES)
    tower[:, LANES:] = right.reshape(PEERS * 16, LANES)
    own = lax.axis_index("x") * Y
    for n in range(NARROW):
        part = got[n % CORE, own + n // CORE].astype(F32)
        grad[n * PART : (n + 1) * PART, 0:LANES] = part[0:PART]
        grad[n * PART : (n + 1) * PART, LANES:] = part[PART : 2 * PART]
    slots = NARROW * PART
    row_grad = grad[...] * 2.0
    square = jnp.mean(row_grad * row_grad, axis=1, keepdims=True)
    at = lax.broadcasted_iota(jnp.int32, (slots, 1), 0)
    picked = [lax.rem(ids[i], rows) for i in range(slots)]
    old = jnp.zeros((slots, 1), F32)
    for i in range(slots):
        old = jnp.where(at == i, accum_at[picked[i]], old)
    new = old + square
    change = LEARN_RATE * row_grad / jnp.sqrt(new)
    new_table[...] = table[...]
    flat = (
        lax.broadcasted_iota(jnp.int32, accum.shape, 0) * LANES
        + lax.broadcasted_iota(jnp.int32, accum.shape, 1)
    )
    sums = accum[...]
    for i in range(slots):
        new_table[pl.ds(picked[i], 1), :] = (
            table[pl.ds(picked[i], 1), :] - change[i : i + 1, :]
        )
        sums = jnp.where(flat == picked[i], new[i : i + 1, :], sums)
    new_accum[...] = sums


def per_device(
    user_feats, tower_weight, table, accum, neg_ids, negative_counts, negative_log_prob, pos_slot
):
    shape = jax.ShapeDtypeStruct
    square = ("x", "yh", "yl")
    smem, hbm = spec(pltpu.SMEM), spec(pltpu.HBM)
    dma = pltpu.SemaphoreType.DMA
    slots = NARROW * PART
    swap = [(0, 1), (1, 0)]
    picked = pl.pallas_call(
        pick_kernel,
        name="pick_rows",
        out_shape=shape((Z, YH * 8 + 8, LANES), BF16),
        in_specs=[smem, smem, spec(), hbm],
        out_specs=spec(),
        scratch_shapes=[
            pltpu.VMEM((YH * PART, 8, 2 * LANES), F32),
            pltpu.VMEM((YH * 8 + 8, LANES), F32),
            dma((YH * PART,)),
        ],
        compiler_params=params(60),
    )(neg_ids, negative_counts, negative_log_prob.reshape(1, -1), table)
    picked = lax.all_to_all(picked, "z", 0, 0, tiled=True)
    spread = pl.pallas_call(
        spread_kernel,
        name="spread_rows",
        out_shape=shape((X * YL, YH * PACK, LANES), BF16),
        in_specs=[spec()],
        out_specs=spec(),
        scratch_shapes=[pltpu.VMEM((YH * PACK, LANES), F32)],
        compiler_params=params(),
    )(picked)
    mine = lax.all_to_all(spread, ("x", "yl"), 0, 0, tiled=True)
    queries = user_feats.shape[0]
    half_slots = SQUARE * ROWS
    feats2 = lax.ppermute(user_feats, "core", swap)
    query = pl.pallas_call(
        query_kernel,
        name="queries",
        out_shape=shape((2 * queries, 2 * LANES), BF16),
        in_specs=[spec()] * 3,
        out_specs=spec(),
        compiler_params=params(),
        cost_estimate=pl.CostEstimate(
            flops=16 * queries * LANES * 4 * LANES, bytes_accessed=2**20, transcendentals=0
        ),
    )(user_feats, feats2, tower_weight)
    expo, columns, stats = pl.pallas_call(
        score_kernel,
        name="scores",
        out_shape=(
            shape((2 * queries, half_slots), F32),
            shape((2 * queries, LANES), F32),
            shape((16, LANES), F32),
        ),
        in_specs=[spec()] * 3,
        out_specs=(spec(),) * 3,
        compiler_params=params(32),
    )(query, pos_slot.reshape(-1, LANES), mine)
    stats = lax.all_gather(stats, "core", axis=0)
    tower_part = (SQUARE, 32, LANES)
    dscore, kept, sent = pl.pallas_call(
        tower_kernel,
        name="tower_gradient",
        out_shape=(
            shape((2 * queries, half_slots), BF16),
            shape(tower_part, F32),
            shape(tower_part, BF16),
        ),
        in_specs=[spec()] * 6,
        out_specs=(spec(),) * 3,
        compiler_params=params(32),
    )(user_feats, feats2, mine, expo, columns, stats)
    got = lax.all_gather(sent, "core", axis=0)
    slot_part = pl.pallas_call(
        slot_kernel,
        name="slot_gradient",
        out_shape=shape((SQUARE, 2 * ROWS, LANES), BF16),
        in_specs=[spec()] * 2,
        out_specs=spec(),
        compiler_params=params(32),
        cost_estimate=pl.CostEstimate(
            flops=8 * queries * half_slots * LANES, bytes_accessed=2**21, transcendentals=0
        ),
    )(dscore, query)
    chip = pl.pallas_call(
        join_kernel,
        name="join_tower",
        out_shape=shape((SQUARE, 2 * ROWS + 32, LANES), BF16),
        in_specs=[spec()] * 3,
        out_specs=spec(),
        compiler_params=params(),
    )(slot_part, kept, got)
    chip = lax.all_to_all(chip, square, 0, 0, tiled=True)
    sums = pl.pallas_call(
        plane_sum_kernel,
        name="plane_sum",
        out_shape=shape((Z, 40, LANES), BF16),
        in_specs=[spec()],
        out_specs=spec(),
        scratch_shapes=[pltpu.VMEM((Z, 40, LANES), F32)],
        compiler_params=params(),
    )(chip)
    sums = lax.all_to_all(sums, "z", 0, 0, tiled=True)
    whole = pl.pallas_call(
        z_sum_kernel,
        name="z_sum",
        out_shape=shape((SQUARE, 40, LANES), BF16),
        in_specs=[spec()],
        out_specs=spec(),
        compiler_params=params(),
    )(sums)
    whole = lax.all_to_all(whole, square, 0, 0, tiled=True)
    whole = lax.all_gather(whole, "core", axis=0)
    new_table, new_accum, tower_grad = pl.pallas_call(
        update_kernel,
        name="row_update",
        out_shape=(
            shape(table.shape, F32),
            shape((8, LANES), F32),
            shape(tower_weight.shape, F32),
        ),
        in_specs=[smem, smem, spec(), spec(), spec()],
        out_specs=(spec(), spec(), spec()),
        scratch_shapes=[pltpu.VMEM((slots, 2 * LANES), F32)],
        compiler_params=params(),
    )(neg_ids, accum, whole, table, accum.reshape(8, LANES))
    return (new_table, new_accum.reshape(-1), tower_grad)


def solution(mesh):
    fine = Mesh(mesh.devices.reshape(X, Z, YH, YL, CORE), ("x", "z", "yh", "yl", "core"))
    wide, narrow = ("x", "z"), ("yh", "yl", "core")
    return jax.shard_map(
        per_device,
        mesh=fine,
        in_specs=(
            P(wide + narrow, None),
            P(),
            P(wide, None),
            P(wide),
            P(wide),
            P(wide),
            P(wide),
            P(wide + narrow),
        ),
        out_specs=(P(wide, None), P(wide), P()),
        check_vma=False,
    )
```
